128 devices in a mesh: ctx: 32 (over z, x, core), hg: 4 (over y).
Axes of the slice: x: 4, y: 4, z: 4, core: 2. Of those that a mesh axis runs over, the one named last changes fastest.
Arguments:
- queries: bfloat16 [8192, 8, 8, 128], P('ctx', 'hg'), may hold values from -6 to 6
- key_vectors: bfloat16 [8192, 8, 128], P('ctx', 'hg'), may hold values from -6 to 6
- value_vectors: bfloat16 [8192, 8, 128], P('ctx', 'hg'), may hold values from -6 to 6
- outputs: bfloat16 [8192, 8, 8, 128], P('ctx', 'hg'), may hold values from -1.796875 to 1.796875
- out_grads: bfloat16 [8192, 8, 8, 128], P('ctx', 'hg'), may hold values from -18 to 18
- log_sums: bfloat16 [8192, 8, 8], P('ctx', 'hg'), may hold values from -0.5 to 14
- head_kind: int32 [8], replicated, may hold values from 0 to 1, as said below
- sink_len: int32 [8], replicated, may hold values from 64 to 128, as said below
- window_len: int32 [8], replicated, may hold values from 128 to 256, as said below
Outputs:
- query_grads: bfloat16 [8192, 8, 8, 128], P('ctx', 'hg')
- key_grads: bfloat16 [8192, 8, 128], P('ctx', 'hg')
- value_grads: bfloat16 [8192, 8, 128], P('ctx', 'hg')
The draws below stay inside these ranges and needn't reach their ends.
Inputs may be any that keep to these rules, and one draw needn't show every extreme that they name: `head_kind`: among KV heads 4m to 4m + 3 exactly two have 1. In every draw some such four hold both of their 1s in heads 4m, 4m + 1 or both in 4m + 2, 4m + 3. `sink_len`: some KV head with head_kind 0 has exactly 128. `window_len`: some KV head with head_kind 0 has exactly 256.
All inputs are finite; a program needn't handle non-finite values.
Results may differ from the reference program's by a relative error of at most 0.005.
Values may be sent and summed in bfloat16 or wider, within the bound.
A program may use at most 64 MiB of HBM per device.

```python
import jax
import jax.numpy as jnp
import numpy as np
from jax import lax

HD = 128
KV_HEADS = 8
QPK = 8
SINK_MAX = 128
WIN_MAX = 256
SEQ = 8192


def head_layout(key):
    pair_count = KV_HEADS // 4
    table = jnp.array(np.array([[1, 1, 0, 0], [0, 0, 1, 1], [1, 0, 1, 0], [1, 0, 0, 1], [0, 1, 1, 0], [0, 1, 0, 1]]), jnp.int32)
    key_list = jax.random.split(key, 7)
    picks = jax.random.randint(key_list[0], (pair_count,), 0, 6)
    forced = jax.random.randint(key_list[1], (), 0, pair_count)
    forced_pick = jax.random.randint(key_list[2], (), 0, 2)
    picks = jnp.where(jnp.arange(pair_count) == forced, forced_pick, picks)
    kinds = table[picks].reshape(KV_HEADS)
    running = jnp.argsort(kinds, stable=True)[:KV_HEADS // 2]
    sinks = jax.random.randint(key_list[3], (KV_HEADS,), SINK_MAX // 2, SINK_MAX + 1)
    sinks = sinks.at[running[jax.random.randint(key_list[4], (), 0, KV_HEADS // 2)]].set(SINK_MAX)
    windows = jax.random.randint(key_list[5], (KV_HEADS,), WIN_MAX // 2, WIN_MAX + 1)
    windows = windows.at[running[jax.random.randint(key_list[6], (), 0, KV_HEADS // 2)]].set(WIN_MAX)
    return (kinds.astype(jnp.int32), sinks.astype(jnp.int32), windows.astype(jnp.int32))


def draw_head_kind(key, part):
    return head_layout(key)[0]


def draw_sink_len(key, part):
    return head_layout(key)[1]


def draw_window_len(key, part):
    return head_layout(key)[2]


def draw_log_sums(key, part):
    kinds, sinks, windows = head_layout(key)
    key = jax.random.fold_in(key, 17)
    row_count = jnp.arange(SEQ, dtype=jnp.float32)[:, None] + 1.0
    window_f = windows.astype(jnp.float32)[None, :]
    sink_f = sinks.astype(jnp.float32)[None, :]
    running_count = jnp.minimum(row_count, window_f) + jnp.maximum(0.0, jnp.minimum(sink_f, row_count - window_f))
    counts = jnp.where(kinds[None, :] == 1, row_count, running_count)
    noise = jax.random.truncated_normal(key, -3.0, 3.0, (SEQ, KV_HEADS, QPK), jnp.float32) * 0.25
    return (jnp.log(counts)[:, :, None] + 0.5 + noise).astype(jnp.bfloat16)


def block_scale(own_key, dims, cuts, low, high):
    loudness = 1.0
    for axis_at, parts in cuts:
        steps = jax.random.uniform(jax.random.fold_in(jax.random.fold_in(own_key, 6), axis_at), (parts,), jnp.float32, low / len(cuts), high / len(cuts))
        loudness = loudness * jnp.repeat(jnp.exp(steps), dims[axis_at] // parts).reshape((-1,) + (1,) * (len(dims) - 1 - axis_at))
    return loudness


def normal_values(key, dims, width, reach, cuts=(), kind=jnp.bfloat16):
    values = jax.random.normal(key, dims, jnp.float32) * width
    if len(cuts) > 0:
        values = block_scale(key, dims, cuts, -0.22, 0.18) * values
    return jnp.clip(values, min=-reach, max=reach).astype(kind)


def setup_inputs(seed: int = 0) -> dict:
    seeds = jax.random.split(jax.random.key(seed), 10)
    return {
        "queries": normal_values(seeds[0], (SEQ, KV_HEADS, QPK, HD), 1.0, 6.0, ((0, 32), (1, 4))),
        "key_vectors": normal_values(seeds[1], (SEQ, KV_HEADS, HD), 1.0, 6.0, ((0, 32), (1, 4))),
        "value_vectors": normal_values(seeds[2], (SEQ, KV_HEADS, HD), 1.0, 6.0, ((0, 32), (1, 4))),
        "outputs": normal_values(seeds[3], (SEQ, KV_HEADS, QPK, HD), 0.3, 1.796875, ((0, 32), (1, 4))),
        "out_grads": normal_values(seeds[4], (SEQ, KV_HEADS, QPK, HD), 3.0, 18.0, ((0, 32), (1, 4))),
        "log_sums": draw_log_sums(jax.random.fold_in(seeds[9], 71), 0),
        "head_kind": draw_head_kind(jax.random.fold_in(seeds[9], 71), 0),
        "sink_len": draw_sink_len(jax.random.fold_in(seeds[9], 71), 0),
        "window_len": draw_window_len(jax.random.fold_in(seeds[9], 71), 0),
    }


def block_grads(query_vecs, grad_vecs, lse_vecs, total_vecs, key_block, value_block, allowed, scaling):
    scores = jnp.einsum("qd,kd->qk", query_vecs, key_block, preferred_element_type=jnp.float32) * scaling
    weights = jnp.where(allowed, jnp.exp(scores - lse_vecs[:, None]), 0.0)
    weights_low = weights.astype(jnp.bfloat16)
    value_part = jnp.einsum("qk,qd->kd", weights_low, grad_vecs, preferred_element_type=jnp.float32)
    weight_grad = jnp.einsum("qd,kd->qk", grad_vecs, value_block, preferred_element_type=jnp.float32)
    score_grad = (weights * (weight_grad - total_vecs[:, None])).astype(jnp.bfloat16)
    query_part = jnp.einsum("qk,kd->qd", score_grad, key_block, preferred_element_type=jnp.float32)
    key_part = jnp.einsum("qk,qd->kd", score_grad, query_vecs, preferred_element_type=jnp.float32)
    return query_part, key_part, value_part


def row_inputs(query_h, grad_h, output_h, lse_h, row_start, length):
    row_end = row_start + length
    query_vecs = query_h[row_start:row_end].reshape(length * QPK, HD)
    grad_vecs = grad_h[row_start:row_end].reshape(length * QPK, HD)
    out_vecs = output_h[row_start:row_end].reshape(length * QPK, HD)
    totals = jnp.sum(grad_vecs.astype(jnp.float32) * out_vecs.astype(jnp.float32), axis=1)
    lse_vecs = lse_h[row_start:row_end].reshape(length * QPK).astype(jnp.float32)
    positions = row_start + jnp.arange(length * QPK, dtype=jnp.int32) // QPK
    return query_vecs, grad_vecs, totals, lse_vecs, positions


def retrieval_head(tensors):
    query_h, key_h, value_h, output_h, grad_h, lse_h = tensors
    scaling = HD ** -0.5
    length = SEQ // 16
    key_sum = jnp.zeros((SEQ, HD), jnp.float32)
    value_sum = jnp.zeros((SEQ, HD), jnp.float32)
    pieces = []
    for row_start in range(0, SEQ, length):
        row_end = row_start + length
        query_vecs, grad_vecs, totals, lse_vecs, positions = row_inputs(query_h, grad_h, output_h, lse_h, row_start, length)
        key_pos = jnp.arange(row_end, dtype=jnp.int32)
        allowed = key_pos[None, :] <= positions[:, None]
        query_part, key_part, value_part = block_grads(query_vecs, grad_vecs, lse_vecs, totals, key_h[:row_end], value_h[:row_end], allowed, scaling)
        pieces.append((query_part * scaling).astype(jnp.bfloat16).reshape(length, QPK, HD))
        key_sum = key_sum.at[:row_end].add(key_part)
        value_sum = value_sum.at[:row_end].add(value_part)
    return jnp.concatenate(pieces, axis=0), (key_sum * scaling).astype(jnp.bfloat16), value_sum.astype(jnp.bfloat16)


def running_head(tensors):
    query_h, key_h, value_h, output_h, grad_h, lse_h, sink_count, window = tensors
    scaling = HD ** -0.5
    length = SEQ // 16
    key_pad = jnp.concatenate([jnp.zeros((WIN_MAX, HD), key_h.dtype), key_h], axis=0)
    value_pad = jnp.concatenate([jnp.zeros((WIN_MAX, HD), value_h.dtype), value_h], axis=0)
    pad_key_sum = jnp.zeros((SEQ + WIN_MAX, HD), jnp.float32)
    pad_value_sum = jnp.zeros((SEQ + WIN_MAX, HD), jnp.float32)
    sink_key_sum = jnp.zeros((SINK_MAX, HD), jnp.float32)
    sink_value_sum = jnp.zeros((SINK_MAX, HD), jnp.float32)
    in_sink = jnp.arange(SINK_MAX + WIN_MAX + length, dtype=jnp.int32) < SINK_MAX
    pieces = []
    for row_start in range(0, SEQ, length):
        row_end = row_start + length
        query_vecs, grad_vecs, totals, lse_vecs, positions = row_inputs(query_h, grad_h, output_h, lse_h, row_start, length)
        key_block = jnp.concatenate([key_h[:SINK_MAX], key_pad[row_start:row_end + WIN_MAX]], axis=0)
        value_block = jnp.concatenate([value_h[:SINK_MAX], value_pad[row_start:row_end + WIN_MAX]], axis=0)
        key_pos = jnp.concatenate([jnp.arange(SINK_MAX, dtype=jnp.int32), row_start - WIN_MAX + jnp.arange(WIN_MAX + length, dtype=jnp.int32)])
        distance = positions[:, None] - key_pos[None, :]
        allowed = jnp.where(in_sink[None, :], (key_pos < sink_count)[None, :] & (distance >= window), (key_pos >= 0)[None, :] & (distance >= 0) & (distance < window))
        query_part, key_part, value_part = block_grads(query_vecs, grad_vecs, lse_vecs, totals, key_block, value_block, allowed, scaling)
        pieces.append((query_part * scaling).astype(jnp.bfloat16).reshape(length, QPK, HD))
        sink_key_sum = sink_key_sum + key_part[:SINK_MAX]
        sink_value_sum = sink_value_sum + value_part[:SINK_MAX]
        pad_key_sum = pad_key_sum.at[row_start:row_end + WIN_MAX].add(key_part[SINK_MAX:])
        pad_value_sum = pad_value_sum.at[row_start:row_end + WIN_MAX].add(value_part[SINK_MAX:])
    key_sum = pad_key_sum[WIN_MAX:].at[:SINK_MAX].add(sink_key_sum)
    value_sum = pad_value_sum[WIN_MAX:].at[:SINK_MAX].add(sink_value_sum)
    return jnp.concatenate(pieces, axis=0), (key_sum * scaling).astype(jnp.bfloat16), value_sum.astype(jnp.bfloat16)


def reference(queries, key_vectors, value_vectors, outputs, out_grads, log_sums, head_kind, sink_len, window_len):
    head_half = KV_HEADS // 2
    retrieval_ids = jnp.argsort(1 - head_kind, stable=True)[:head_half].astype(jnp.int32)
    running_ids = jnp.argsort(head_kind, stable=True)[:head_half].astype(jnp.int32)

    def select_heads(chosen):
        return tuple(jnp.moveaxis(jnp.take(tensor_in, chosen, axis=1), 1, 0) for tensor_in in (queries, key_vectors, value_vectors, outputs, out_grads, log_sums))

    retrieval_out = lax.map(retrieval_head, select_heads(retrieval_ids))
    running_out = lax.map(running_head, select_heads(running_ids) + (jnp.take(sink_len, running_ids), jnp.take(window_len, running_ids)))
    shapes = (queries.shape, key_vectors.shape, value_vectors.shape)
    results = []
    for output_index in range(3):
        assembled = jnp.zeros(shapes[output_index], jnp.bfloat16)
        assembled = assembled.at[:, retrieval_ids].set(jnp.moveaxis(retrieval_out[output_index], 0, 1))
        assembled = assembled.at[:, running_ids].set(jnp.moveaxis(running_out[output_index], 0, 1))
        results.append(assembled)
    return (results[0], results[1], results[2])
```

```python
import functools

import jax
import jax.numpy as jnp
from jax import lax
from jax.experimental import pallas as pl
from jax.experimental.pallas import tpu as pltpu
from jax.sharding import PartitionSpec as P

SINK = 128
MESH = pl.DeviceIdType.MESH
LOG2E = 1.4426950408889634
f32 = jnp.float32
bf16 = jnp.bfloat16


def dot(a, b):
    return lax.dot_general(a, b, (((1,), (0,)), ((), ())), preferred_element_type=f32)


def kernel(
    n,
    kind,
    sinks,
    windows,
    q_in,
    kv_in,
    do_in,
    aux_in,
    dq_out,
    dkv_out,
    q3,
    do3,
    kv3,
    aux3,
    kv_all,
    part,
    rpart,
    band_kv,
    halo,
    sink,
    sink_send,
    sink_recv,
    back_send,
    back_recv,
    q_t,
    do_t,
    q_r,
    do_r,
    aux_r,
    dq_t,
    dq_band,
    dq_near,
    dq_away,
    dq_home,
    dkv_own,
    dkv_band,
    dkv_near,
    dkv_away,
    dkv_home,
    local_sem,
    swap_send,
    swap_recv,
    kv_send,
    kv_recv,
    part_send,
    part_recv,
    sink_ss,
    sink_rs,
    sgrad_ss,
    sgrad_rs,
    edge_sem,
):
    tok = kv_all.shape[2]
    heads = q_in.shape[2]
    hd = q_in.shape[3]
    rows = tok * heads
    scale = hd ** (-0.5)
    me = lax.axis_index("ctx")
    g = lax.axis_index("hg")
    pg = g + 1 - 2 * lax.rem(g, 2)

    def remote(src, dst, ss, rs, ctx, hg):
        return pltpu.make_async_remote_copy(
            src_ref=src, dst_ref=dst, send_sem=ss, recv_sem=rs, device_id=(ctx, hg), device_id_type=MESH
        )

    local = []
    for slot in range(2):
        local.append((kv_in.at[slot], kv3.at[slot]))
        local.append((q_in.at[:, slot], q3.at[slot]))
        local.append((do_in.at[:, slot], do3.at[slot]))
        local.append((aux_in.at[slot], aux3.at[slot]))
    local = [pltpu.make_async_copy(a, b, local_sem.at[i]) for i, (a, b) in enumerate(local)]
    for c in local:
        c.start()

    barrier = pltpu.get_barrier_semaphore()

    def greet(s, _):
        pl.semaphore_signal(barrier, inc=1, device_id=(lax.rem(me + s, n), g), device_id_type=MESH)
        return 0

    pl.semaphore_signal(barrier, inc=1, device_id=(me, pg), device_id_type=MESH)
    lax.fori_loop(1, n, greet, 0)
    pl.semaphore_wait(barrier, n)

    swaps = [
        remote(kv_in.at[1], kv3.at[2], swap_send.at[0], swap_recv.at[0], me, pg),
        remote(aux_in.at[1], aux3.at[2], swap_send.at[1], swap_recv.at[1], me, pg),
        remote(q_in.at[:, 1], q3.at[2], swap_send.at[2], swap_recv.at[2], me, pg),
        remote(do_in.at[:, 1], do3.at[2], swap_send.at[3], swap_recv.at[3], me, pg),
    ]
    for c in swaps:
        c.start()

    first_ret = kind[2 * g] == 1
    pair = kind[2 * g] + kind[2 * g + 1] == 1
    other_slot = jnp.where(pair, 1, 2)
    full_slot = jnp.where(first_ret, 0, other_slot)
    band_slot = jnp.where(first_ret, other_slot, 0)
    other_id = jnp.where(pair, 2 * g + 1, 2 * pg + 1)
    band_id = jnp.where(first_ret, other_id, 2 * g)
    sink_count = sinks[band_id]
    window = windows[band_id]

    for c in local:
        c.wait()
    swaps[0].wait_recv()
    kv_all[me] = kv3[full_slot]
    band_kv[...] = kv3[band_slot]

    def kv_copy(block, dst):
        return remote(kv_all.at[block], kv_all.at[block], kv_send.at[dst], kv_recv.at[block], dst, g)

    def sink_copy(dst):
        return remote(band_kv.at[:, pl.ds(0, SINK)], sink, sink_ss.at[dst], sink_rs, dst, g)

    halo_copy = remote(band_kv, halo, edge_sem.at[0], edge_sem.at[1], lax.rem(me + 1, n), g)

    @pl.when(me < n - 1)
    def _():
        halo_copy.start()

    @pl.when(me == 0)
    def _():
        halo[...] = jnp.zeros_like(halo)
        sink[...] = band_kv[:, pl.ds(0, SINK)]

        def send(dst, _):
            sink_copy(dst).start()
            return 0

        lax.fori_loop(1, n, send, 0)

    def send_kv(dst, _):
        kv_copy(me, dst).start()
        return 0

    lax.fori_loop(me + 1, n, send_kv, 0)

    for c in swaps[1:]:
        c.wait_recv()

    def load_head(slot):
        q = q3[slot].reshape(rows, hd)
        d = do3[slot].reshape(rows, hd)
        q_r[...] = q
        do_r[...] = d
        q_t[...] = q.T
        do_t[...] = d.T
        aux_r[...] = aux3[slot]

    def block(k, v, allowed):
        s = dot(k, q_t[...])
        p = jnp.exp2(s * (scale * LOG2E) - aux_r[0:1, :])
        if allowed is not None:
            p = jnp.where(allowed, p, 0.0)
        dp = dot(v, do_t[...])
        ds = (p * (dp - aux_r[1:2, :])).astype(bf16)
        dv = dot(p.astype(bf16), do_r[...])
        dk = dot(ds, q_r[...])
        dq_t[...] += dot(k.T, ds)
        return dk * scale, dv

    def positions(count):
        key = lax.broadcasted_iota(jnp.int32, (count, rows), 0)
        row = lax.broadcasted_iota(jnp.int32, (count, rows), 1) // heads
        return key, row

    load_head(band_slot)
    dq_t[...] = jnp.zeros_like(dq_t)
    key, row = positions(tok)
    gap = row - key
    dk, dv = block(band_kv[0], band_kv[1], (gap >= 0) & (gap < window))
    dkv_band[0] = dk
    dkv_band[1] = dv

    @pl.when(me > 0)
    def _():
        halo_copy.wait_recv()
        sink_copy(0).wait_recv()

    dk, dv = block(halo[0], halo[1], (gap < window - tok) & (me > 0))
    back_send[0] = dk.astype(bf16)
    back_send[1] = dv.astype(bf16)
    back_copy = remote(back_send, back_recv, edge_sem.at[2], edge_sem.at[3], lax.rem(me + n - 1, n), g)

    @pl.when(me > 0)
    def _():
        back_copy.start()

    key, row = positions(SINK)
    dk, dv = block(sink[0], sink[1], (key < sink_count) & (row - key >= window - me * tok))
    sink_send[0] = dk.astype(bf16)
    sink_send[1] = dv.astype(bf16)

    def sgrad_copy(src):
        return remote(sink_send, sink_recv.at[src], sgrad_ss, sgrad_rs.at[src], 0, g)

    @pl.when(me > 0)
    def _():
        sgrad_copy(me).start()

    @pl.when(me == 0)
    def _():
        dkv_band[:, pl.ds(0, SINK)] += jnp.stack([dk, dv])

    dq_band[...] = (dq_t[...] * scale).T.astype(bf16)

    load_head(full_slot)
    dq_t[...] = jnp.zeros_like(dq_t)
    key, row = positions(tok)
    dk, dv = block(kv_all[me, 0], kv_all[me, 1], key <= row)
    dkv_own[0] = dk
    dkv_own[1] = dv

    def part_copy(blk, src):
        return remote(part.at[blk], rpart.at[src], part_send.at[blk], part_recv.at[src], blk, g)

    def step(s, _):
        j = me - s
        kv_copy(j, me).wait_recv()
        dk, dv = block(kv_all[j, 0], kv_all[j, 1], None)
        part[j, 0] = dk.astype(bf16)
        part[j, 1] = dv.astype(bf16)
        part_copy(j, me).start()
        return 0

    lax.fori_loop(1, me + 1, step, 0)

    dq_full = (dq_t[...] * scale).T.astype(bf16)
    band = dq_band[...]
    dq_near[...] = jnp.where(first_ret, dq_full, band).reshape(tok, heads, hd)
    dq_away[...] = jnp.where(first_ret, band, dq_full).reshape(tok, heads, hd)
    back_q = remote(dq_away, dq_home, swap_send.at[4], swap_recv.at[4], me, pg)
    back_q.start()
    out_near = pltpu.make_async_copy(dq_near, dq_out.at[:, 0], local_sem.at[0])
    out_near.start()

    @pl.when(me < n - 1)
    def _():
        back_copy.wait_recv()
        dkv_band[...] += back_recv[...].astype(f32)

    @pl.when(me == 0)
    def _():
        def add(src, _):
            sgrad_copy(src).wait_recv()
            dkv_band[:, pl.ds(0, SINK)] += sink_recv[src].astype(f32)
            return 0

        lax.fori_loop(1, n, add, 0)

    def add(src, _):
        part_copy(me, src).wait_recv()
        dkv_own[...] += rpart[src].astype(f32)
        return 0

    lax.fori_loop(me + 1, n, add, 0)

    full = dkv_own[...].astype(bf16)
    band = dkv_band[...].astype(bf16)
    dkv_near[...] = jnp.where(first_ret, full, band)
    dkv_away[...] = jnp.where(first_ret, band, full)
    back_kv = remote(dkv_away, dkv_home, swap_send.at[5], swap_recv.at[5], me, pg)
    back_kv.start()
    dkv_out[0] = dkv_near[...]

    back_q.wait()
    dq_home[...] = jnp.where(pair, dq_away[...], dq_home[...])
    out_far = pltpu.make_async_copy(dq_home, dq_out.at[:, 1], local_sem.at[1])
    out_far.start()
    back_kv.wait()
    dkv_out[1] = jnp.where(pair, dkv_away[...], dkv_home[...])

    for c in swaps:
        c.wait_send()

    def drain_kv(dst, _):
        kv_copy(me, dst).wait_send()
        return 0

    lax.fori_loop(me + 1, n, drain_kv, 0)

    def drain_part(blk, _):
        part_copy(blk, me).wait_send()
        return 0

    lax.fori_loop(0, me, drain_part, 0)

    @pl.when(me < n - 1)
    def _():
        halo_copy.wait_send()

    @pl.when(me > 0)
    def _():
        back_copy.wait_send()
        sgrad_copy(me).wait_send()

    @pl.when(me == 0)
    def _():
        def drain(dst, _):
            sink_copy(dst).wait_send()
            return 0

        lax.fori_loop(1, n, drain, 0)

    out_near.wait()
    out_far.wait()


def shards(queries, keys, values, outputs, grads, logs, kind, sinks, windows):
    tok, _, heads, hd = queries.shape
    rows = tok * heads
    n = lax.axis_size("ctx")
    delta = jnp.sum(grads.astype(f32) * outputs.astype(f32), axis=-1)
    lse = logs.astype(f32) * LOG2E
    aux = jnp.stack([lse, delta], axis=0)
    aux = jnp.moveaxis(aux, 2, 0).reshape(2, 2, rows)
    aux = jnp.pad(aux, ((0, 0), (0, 6), (0, 0)))
    kv = jnp.moveaxis(jnp.stack([keys, values], axis=0), 2, 0)
    smem = pl.BlockSpec(memory_space=pltpu.SMEM)
    hbm = pl.BlockSpec(memory_space=pl.ANY)
    vmem = pl.BlockSpec(memory_space=pltpu.VMEM)
    V = pltpu.VMEM
    dma = pltpu.SemaphoreType.DMA
    dq, dkv = pl.pallas_call(
        functools.partial(kernel, n),
        in_specs=[smem, smem, smem, hbm, hbm, hbm, hbm],
        out_specs=[hbm, vmem],
        out_shape=[
            jax.ShapeDtypeStruct((tok, 2, heads, hd), bf16),
            jax.ShapeDtypeStruct((2, 2, tok, hd), bf16),
        ],
        scratch_shapes=[
            V((3, tok, heads, hd), bf16),
            V((3, tok, heads, hd), bf16),
            V((3, 2, tok, hd), bf16),
            V((3, 8, rows), f32),
            V((n, 2, tok, hd), bf16),
            V((n, 2, tok, hd), bf16),
            V((n, 2, tok, hd), bf16),
            V((2, tok, hd), bf16),
            V((2, tok, hd), bf16),
            V((2, SINK, hd), bf16),
            V((2, SINK, hd), bf16),
            V((n, 2, SINK, hd), bf16),
            V((2, tok, hd), bf16),
            V((2, tok, hd), bf16),
            V((hd, rows), bf16),
            V((hd, rows), bf16),
            V((rows, hd), bf16),
            V((rows, hd), bf16),
            V((8, rows), f32),
            V((hd, rows), f32),
            V((rows, hd), bf16),
            V((tok, heads, hd), bf16),
            V((tok, heads, hd), bf16),
            V((tok, heads, hd), bf16),
            V((2, tok, hd), f32),
            V((2, tok, hd), f32),
            V((2, tok, hd), bf16),
            V((2, tok, hd), bf16),
            V((2, tok, hd), bf16),
            dma((8,)),
            dma((6,)),
            dma((6,)),
            dma((n,)),
            dma((n,)),
            dma((n,)),
            dma((n,)),
            dma((n,)),
            dma,
            dma,
            dma((n,)),
            dma((4,)),
        ],
        compiler_params=pltpu.CompilerParams(
            collective_id=0, has_side_effects=True, vmem_limit_bytes=60 * 2**20
        ),
        name="attention_grads",
    )(kind, sinks, windows, queries, kv, grads, aux)
    dkv = jnp.moveaxis(dkv, 0, 2)
    return dq, dkv[0], dkv[1]


def solution(mesh):
    return jax.shard_map(
        shards,
        mesh=mesh,
        in_specs=(
            P("ctx", "hg", None, None),
            P("ctx", "hg", None),
            P("ctx", "hg", None),
            P("ctx", "hg", None, None),
            P("ctx", "hg", None, None),
            P("ctx", "hg", None),
            P(),
            P(),
            P(),
        ),
        out_specs=(P("ctx", "hg", None, None), P("ctx", "hg", None), P("ctx", "hg", None)),
        check_vma=False,
    )
```

```python
import functools

import jax
import jax.numpy as jnp
from jax import lax
from jax.experimental import pallas as pl
from jax.experimental.pallas import tpu as pltpu
from jax.sharding import PartitionSpec as P

SINK = 128
AHEAD = 4
MESH = pl.DeviceIdType.MESH
LOG2E = 1.4426950408889634
f32 = jnp.float32
bf16 = jnp.bfloat16


def dot(a, b):
    return lax.dot_general(a, b, (((1,), (0,)), ((), ())), preferred_element_type=f32)


def kernel(
    n,
    kind,
    sinks,
    windows,
    q_in,
    kv_in,
    do_in,
    aux_in,
    dq_out,
    dkv_out,
    q3,
    do3,
    kv3,
    aux3,
    kv_all,
    part,
    rpart,
    spart,
    pown,
    band_kv,
    halo,
    sink,
    sink_send,
    sink_recv,
    back_send,
    back_recv,
    q_t,
    do_t,
    q_r,
    do_r,
    aux_r,
    dq_t,
    dq_band,
    dq_near,
    dq_away,
    dq_home,
    dkv_own,
    dkv_band,
    dkv_near,
    dkv_away,
    dkv_home,
    local_sem,
    swap_send,
    swap_recv,
    kv_send,
    kv_recv,
    fwd_send,
    part_send,
    part_recv,
    spart_recv,
    sink_ss,
    sink_rs,
    sgrad_ss,
    sgrad_rs,
    edge_sem,
):
    tok = kv_all.shape[2]
    heads = q_in.shape[2]
    hd = q_in.shape[3]
    rows = tok * heads
    scale = hd ** (-0.5)
    me = lax.axis_index("ctx")
    g = lax.axis_index("hg")
    pg = g + 1 - 2 * lax.rem(g, 2)
    chips = n // 2
    chip = me // 2
    core = lax.rem(me, 2)
    sib = me + 1 - 2 * core

    def remote(src, dst, ss, rs, ctx, hg):
        return pltpu.make_async_remote_copy(
            src_ref=src, dst_ref=dst, send_sem=ss, recv_sem=rs, device_id=(ctx, hg), device_id_type=MESH
        )

    local = []
    for slot in range(2):
        local.append((kv_in.at[slot], kv3.at[slot]))
        local.append((q_in.at[:, slot], q3.at[slot]))
        local.append((do_in.at[:, slot], do3.at[slot]))
        local.append((aux_in.at[slot], aux3.at[slot]))
    local = [pltpu.make_async_copy(a, b, local_sem.at[i]) for i, (a, b) in enumerate(local)]
    for c in local:
        c.start()

    barrier = pltpu.get_barrier_semaphore()

    def greet(s, _):
        pl.semaphore_signal(barrier, inc=1, device_id=(lax.rem(me + s, n), g), device_id_type=MESH)
        return 0

    pl.semaphore_signal(barrier, inc=1, device_id=(me, pg), device_id_type=MESH)
    lax.fori_loop(1, n, greet, 0)
    pl.semaphore_wait(barrier, n)

    swaps = [
        remote(kv_in.at[1], kv3.at[2], swap_send.at[0], swap_recv.at[0], me, pg),
        remote(aux_in.at[1], aux3.at[2], swap_send.at[1], swap_recv.at[1], me, pg),
        remote(q_in.at[:, 1], q3.at[2], swap_send.at[2], swap_recv.at[2], me, pg),
        remote(do_in.at[:, 1], do3.at[2], swap_send.at[3], swap_recv.at[3], me, pg),
    ]
    for c in swaps:
        c.start()

    first_ret = kind[2 * g] == 1
    pair = kind[2 * g] + kind[2 * g + 1] == 1
    other_slot = jnp.where(pair, 1, 2)
    full_slot = jnp.where(first_ret, 0, other_slot)
    band_slot = jnp.where(first_ret, other_slot, 0)
    other_id = jnp.where(pair, 2 * g + 1, 2 * pg + 1)
    band_id = jnp.where(first_ret, other_id, 2 * g)
    sink_count = sinks[band_id]
    window = windows[band_id]

    for c in local:
        c.wait()
    swaps[0].wait_recv()
    kv_all[me] = kv3[full_slot]
    band_kv[...] = kv3[band_slot]

    def kv_copy(block, dst):
        return remote(kv_all.at[block], kv_all.at[block], kv_send.at[dst], kv_recv.at[block], dst, g)

    def sink_copy(dst):
        return remote(band_kv.at[:, pl.ds(0, SINK)], sink, sink_ss.at[dst], sink_rs, dst, g)

    halo_copy = remote(band_kv, halo, edge_sem.at[0], edge_sem.at[1], lax.rem(me + 1, n), g)

    @pl.when(me < n - 1)
    def _():
        halo_copy.start()

    @pl.when(me == 0)
    def _():
        halo[...] = jnp.zeros_like(halo)
        sink[...] = band_kv[:, pl.ds(0, SINK)]

        def send(dst, _):
            sink_copy(dst).start()
            return 0

        lax.fori_loop(1, n, send, 0)

    @pl.when(core == 0)
    def _():
        kv_copy(me, sib).start()

    def send_kv(at, _):
        kv_copy(me, 2 * at + core).start()
        return 0

    lax.fori_loop(chip + 1, chips, send_kv, 0)

    def forward_copy(at):
        blk = 2 * at + core
        return remote(kv_all.at[blk], kv_all.at[blk], fwd_send.at[at], kv_recv.at[blk], sib, g)

    def forward(i, _):
        at = chip - 1 - i
        kv_copy(2 * at + core, me).wait_recv()
        forward_copy(at).start()
        return 0

    lax.fori_loop(0, jnp.minimum(AHEAD, chip), forward, 0)

    for c in swaps[1:]:
        c.wait_recv()

    def load_head(slot):
        q = q3[slot].reshape(rows, hd)
        d = do3[slot].reshape(rows, hd)
        q_r[...] = q
        do_r[...] = d
        q_t[...] = q.T
        do_t[...] = d.T
        aux_r[...] = aux3[slot]

    def block(k, v, allowed):
        s = dot(k, q_t[...])
        p = jnp.exp2(s * (scale * LOG2E) - aux_r[0:1, :])
        if allowed is not None:
            p = jnp.where(allowed, p, 0.0)
        dp = dot(v, do_t[...])
        ds = (p * (dp - aux_r[1:2, :])).astype(bf16)
        dv = dot(p.astype(bf16), do_r[...])
        dk = dot(ds, q_r[...])
        dq_t[...] += dot(k.T, ds)
        return dk * scale, dv

    def positions(count):
        key = lax.broadcasted_iota(jnp.int32, (count, rows), 0)
        row = lax.broadcasted_iota(jnp.int32, (count, rows), 1) // heads
        return key, row

    load_head(band_slot)
    dq_t[...] = jnp.zeros_like(dq_t)
    key, row = positions(tok)
    gap = row - key
    dk, dv = block(band_kv[0], band_kv[1], (gap >= 0) & (gap < window))
    dkv_band[0] = dk
    dkv_band[1] = dv

    @pl.when(me > 0)
    def _():
        halo_copy.wait_recv()
        sink_copy(0).wait_recv()

    dk, dv = block(halo[0], halo[1], (gap < window - tok) & (me > 0))
    back_send[0] = dk.astype(bf16)
    back_send[1] = dv.astype(bf16)
    back_copy = remote(back_send, back_recv, edge_sem.at[2], edge_sem.at[3], lax.rem(me + n - 1, n), g)

    @pl.when(me > 0)
    def _():
        back_copy.start()

    key, row = positions(SINK)
    dk, dv = block(sink[0], sink[1], (key < sink_count) & (row - key >= window - me * tok))
    sink_send[0] = dk.astype(bf16)
    sink_send[1] = dv.astype(bf16)

    def sgrad_copy(src):
        return remote(sink_send, sink_recv.at[src], sgrad_ss, sgrad_rs.at[src], 0, g)

    @pl.when(me > 0)
    def _():
        sgrad_copy(me).start()

    @pl.when(me == 0)
    def _():
        dkv_band[:, pl.ds(0, SINK)] += jnp.stack([dk, dv])

    dq_band[...] = (dq_t[...] * scale).T.astype(bf16)

    load_head(full_slot)
    dq_t[...] = jnp.zeros_like(dq_t)
    key, row = positions(tok)
    dk, dv = block(kv_all[me, 0], kv_all[me, 1], key <= row)
    dkv_own[0] = dk
    dkv_own[1] = dv

    def part_copy(blk, src):
        return remote(part.at[blk], rpart.at[src], part_send.at[blk], part_recv.at[src], blk, g)

    def spart_copy(at):
        blk = 2 * at + 1 - core
        return remote(part.at[blk], spart.at[at], part_send.at[blk], spart_recv.at[at], sib, g)

    @pl.when(core == 1)
    def _():
        kv_copy(sib, me).wait_recv()
        dk, dv = block(kv_all[sib, 0], kv_all[sib, 1], None)
        part[sib, 0] = dk.astype(bf16)
        part[sib, 1] = dv.astype(bf16)
        part_copy(sib, me).start()

    def combine(at):
        blk = 2 * at + core
        spart_copy(at).wait_recv()
        part[blk] = (pown[at] + spart[at].astype(f32)).astype(bf16)
        part_copy(blk, me).start()

    def step(t, _):
        at = chip - t
        mine = 2 * at + core
        theirs = 2 * at + 1 - core

        @pl.when(t - 1 + AHEAD < chip)
        def _():
            forward(t - 1 + AHEAD, 0)

        kv_copy(theirs, me).wait_recv()
        dk, dv = block(kv_all[theirs, 0], kv_all[theirs, 1], None)
        part[theirs, 0] = dk.astype(bf16)
        part[theirs, 1] = dv.astype(bf16)
        spart_copy(at).start()
        dk, dv = block(kv_all[mine, 0], kv_all[mine, 1], None)
        pown[at, 0] = dk
        pown[at, 1] = dv

        @pl.when(t > 1)
        def _():
            combine(at + 1)

        return 0

    lax.fori_loop(1, chip + 1, step, 0)

    @pl.when(chip > 0)
    def _():
        combine(0)

    dq_full = (dq_t[...] * scale).T.astype(bf16)
    band = dq_band[...]
    dq_near[...] = jnp.where(first_ret, dq_full, band).reshape(tok, heads, hd)
    dq_away[...] = jnp.where(first_ret, band, dq_full).reshape(tok, heads, hd)
    back_q = remote(dq_away, dq_home, swap_send.at[4], swap_recv.at[4], me, pg)
    back_q.start()
    out_near = pltpu.make_async_copy(dq_near, dq_out.at[:, 0], local_sem.at[0])
    out_near.start()

    @pl.when(me < n - 1)
    def _():
        back_copy.wait_recv()
        dkv_band[...] += back_recv[...].astype(f32)

    @pl.when(me == 0)
    def _():
        def add(src, _):
            sgrad_copy(src).wait_recv()
            dkv_band[:, pl.ds(0, SINK)] += sink_recv[src].astype(f32)
            return 0

        lax.fori_loop(1, n, add, 0)

    def take(src):
        part_copy(me, src).wait_recv()
        dkv_own[...] += rpart[src].astype(f32)

    @pl.when(core == 0)
    def _():
        take(sib)

    def add(at, _):
        take(2 * at + core)
        return 0

    lax.fori_loop(chip + 1, chips, add, 0)

    full = dkv_own[...].astype(bf16)
    band = dkv_band[...].astype(bf16)
    dkv_near[...] = jnp.where(first_ret, full, band)
    dkv_away[...] = jnp.where(first_ret, band, full)
    back_kv = remote(dkv_away, dkv_home, swap_send.at[5], swap_recv.at[5], me, pg)
    back_kv.start()
    dkv_out[0] = dkv_near[...]

    back_q.wait()
    dq_home[...] = jnp.where(pair, dq_away[...], dq_home[...])
    out_far = pltpu.make_async_copy(dq_home, dq_out.at[:, 1], local_sem.at[1])
    out_far.start()
    back_kv.wait()
    dkv_out[1] = jnp.where(pair, dkv_away[...], dkv_home[...])

    for c in swaps:
        c.wait_send()

    @pl.when(core == 0)
    def _():
        kv_copy(me, sib).wait_send()

    def drain_kv(at, _):
        kv_copy(me, 2 * at + core).wait_send()
        return 0

    lax.fori_loop(chip + 1, chips, drain_kv, 0)

    def drain_forward(at, _):
        forward_copy(at).wait_send()
        return 0

    lax.fori_loop(0, chip, drain_forward, 0)

    def drain_part(blk, _):
        part_copy(blk, me).wait_send()
        return 0

    lax.fori_loop(0, me, drain_part, 0)

    @pl.when(me < n - 1)
    def _():
        halo_copy.wait_send()

    @pl.when(me > 0)
    def _():
        back_copy.wait_send()
        sgrad_copy(me).wait_send()

    @pl.when(me == 0)
    def _():
        def drain(dst, _):
            sink_copy(dst).wait_send()
            return 0

        lax.fori_loop(1, n, drain, 0)

    out_near.wait()
    out_far.wait()


def shards(queries, keys, values, outputs, grads, logs, kind, sinks, windows):
    tok, _, heads, hd = queries.shape
    rows = tok * heads
    n = lax.axis_size("ctx")
    delta = jnp.sum(grads.astype(f32) * outputs.astype(f32), axis=-1)
    lse = logs.astype(f32) * LOG2E
    aux = jnp.stack([lse, delta], axis=0)
    aux = jnp.moveaxis(aux, 2, 0).reshape(2, 2, rows)
    kv = jnp.moveaxis(jnp.stack([keys, values], axis=0), 2, 0)
    smem = pl.BlockSpec(memory_space=pltpu.SMEM)
    hbm = pl.BlockSpec(memory_space=pl.ANY)
    vmem = pl.BlockSpec(memory_space=pltpu.VMEM)
    V = pltpu.VMEM
    dma = pltpu.SemaphoreType.DMA
    dq, dkv = pl.pallas_call(
        functools.partial(kernel, n),
        in_specs=[smem, smem, smem, hbm, hbm, hbm, hbm],
        out_specs=[hbm, vmem],
        out_shape=[
            jax.ShapeDtypeStruct((tok, 2, heads, hd), bf16),
            jax.ShapeDtypeStruct((2, 2, tok, hd), bf16),
        ],
        scratch_shapes=[
            V((3, tok, heads, hd), bf16),
            V((3, tok, heads, hd), bf16),
            V((3, 2, tok, hd), bf16),
            V((3, 2, rows), f32),
            V((n, 2, tok, hd), bf16),
            V((n, 2, tok, hd), bf16),
            V((n, 2, tok, hd), bf16),
            V((n // 2, 2, tok, hd), bf16),
            V((n // 2, 2, tok, hd), f32),
            V((2, tok, hd), bf16),
            V((2, tok, hd), bf16),
            V((2, SINK, hd), bf16),
            V((2, SINK, hd), bf16),
            V((n, 2, SINK, hd), bf16),
            V((2, tok, hd), bf16),
            V((2, tok, hd), bf16),
            V((hd, rows), bf16),
            V((hd, rows), bf16),
            V((rows, hd), bf16),
            V((rows, hd), bf16),
            V((2, rows), f32),
            V((hd, rows), f32),
            V((rows, hd), bf16),
            V((tok, heads, hd), bf16),
            V((tok, heads, hd), bf16),
            V((tok, heads, hd), bf16),
            V((2, tok, hd), f32),
            V((2, tok, hd), f32),
            V((2, tok, hd), bf16),
            V((2, tok, hd), bf16),
            V((2, tok, hd), bf16),
            dma((8,)),
            dma((6,)),
            dma((6,)),
            dma((n,)),
            dma((n,)),
            dma((n // 2,)),
            dma((n,)),
            dma((n,)),
            dma((n // 2,)),
            dma((n,)),
            dma,
            dma,
            dma((n,)),
            dma((4,)),
        ],
        compiler_params=pltpu.CompilerParams(
            collective_id=0, has_side_effects=True, vmem_limit_bytes=60 * 2**20
        ),
        name="attention_grads",
    )(kind, sinks, windows, queries, kv, grads, aux)
    dkv = jnp.moveaxis(dkv, 0, 2)
    return dq, dkv[0], dkv[1]


def solution(mesh):
    return jax.shard_map(
        shards,
        mesh=mesh,
        in_specs=(
            P("ctx", "hg", None, None),
            P("ctx", "hg", None),
            P("ctx", "hg", None),
            P("ctx", "hg", None, None),
            P("ctx", "hg", None, None),
            P("ctx", "hg", None),
            P(),
            P(),
            P(),
        ),
        out_specs=(P("ctx", "hg", None, None), P("ctx", "hg", None), P("ctx", "hg", None)),
        check_vma=False,
    )
```

```python
import functools

import jax
import jax.numpy as jnp
from jax import lax
from jax.experimental import pallas as pl
from jax.experimental.pallas import tpu as pltpu
from jax.sharding import PartitionSpec as P

SINK = 128
MESH = pl.DeviceIdType.MESH
LOG2E = 1.4426950408889634
f32 = jnp.float32
bf16 = jnp.bfloat16


def dot(a, b):
    return lax.dot_general(a, b, (((1,), (0,)), ((), ())), preferred_element_type=f32)


def kernel(
    n,
    kind,
    sinks,
    windows,
    q_in,
    kv_in,
    do_in,
    aux_in,
    dq_out,
    dkv_out,
    q3,
    do3,
    kv3,
    aux3,
    kv_all,
    pown,
    part,
    x_part,
    hop_part,
    z_part,
    sib_part,
    spart,
    halo,
    sink,
    sink_sum,
    sink_send,
    sink_recv,
    back_send,
    back_recv,
    q_t,
    do_t,
    q_r,
    do_r,
    dq_t,
    dq_band,
    dq_full,
    dq_near,
    dq_home,
    dkv_own,
    dkv_band,
    dkv_full,
    dkv_home,
    local_sem,
    swap_send,
    swap_recv,
    kv_recv,
    z_send,
    x_send,
    relay_send,
    fwd_send,
    part_send,
    x_recv,
    hop_recv,
    z_recv,
    sib_recv,
    spart_recv,
    sink_zs,
    sink_xs,
    sink_fs,
    sink_rs,
    sgrad_ss,
    sgrad_rs,
    edge_sem,
):
    tok = kv_all.shape[2]
    heads = q_in.shape[2]
    hd = q_in.shape[3]
    rows = tok * heads
    scale = hd ** (-0.5)
    me = lax.axis_index("ctx")
    g = lax.axis_index("hg")
    pg = g + 1 - 2 * lax.rem(g, 2)
    chips = n // 2
    chip = me // 2
    core = lax.rem(me, 2)
    nx = min(4, chips)
    nz = chips // nx
    z = chip // nx
    x = lax.rem(chip, nx)
    turn = 1 - 2 * core
    sib = me + turn
    beside = lax.rem(me - turn + n, n)
    after = lax.rem(me + 1, n)
    before = lax.rem(me + n - 1, n)

    def remote(src, dst, ss, rs, ctx, hg):
        return pltpu.make_async_remote_copy(
            src_ref=src, dst_ref=dst, send_sem=ss, recv_sem=rs, device_id=(ctx, hg), device_id_type=MESH
        )

    def at_place(pz, px, pc):
        return (pz * nx + px) * 2 + pc

    def loop(lo, hi, body):
        def one(i, _):
            body(i)
            return 0

        lax.fori_loop(lo, hi, one, 0)

    local = []
    for slot in range(2):
        local.append((kv_in.at[slot], kv3.at[slot]))
        local.append((q_in.at[:, slot], q3.at[slot]))
        local.append((do_in.at[:, slot], do3.at[slot]))
        local.append((aux_in.at[slot], aux3.at[slot]))
    local = [pltpu.make_async_copy(a, b, local_sem.at[i]) for i, (a, b) in enumerate(local)]
    for c in local:
        c.start()

    barrier = pltpu.get_barrier_semaphore()

    def greet(ctx, hg):
        pl.semaphore_signal(barrier, inc=1, device_id=(ctx, hg), device_id_type=MESH)

    greet(me, pg)
    greet(sib, g)
    greet(beside, g)
    for d in range(1, nz):
        greet(at_place(lax.rem(z + d, nz), x, core), g)
    for d in range(1, nx):
        greet(at_place(z, lax.rem(x + d, nx), core), g)
    pl.semaphore_wait(barrier, 1 + nz + nx)

    pieces = [
        (kv_in.at[1], kv3.at[2]),
        (aux_in.at[1], aux3.at[2]),
        (q_in.at[:, 1], q3.at[2]),
        (do_in.at[:, 1], do3.at[2]),
    ]
    swaps = [remote(a, b, swap_send.at[i], swap_recv.at[i], me, pg) for i, (a, b) in enumerate(pieces)]
    for c in swaps:
        c.start()

    kinds = [kind[2 * g], kind[2 * g + 1]]
    first_ret = kinds[0] == 1
    second_ret = kinds[1] == 1
    pair = kinds[0] + kinds[1] == 1
    full_slot = jnp.where(first_ret, 0, jnp.where(pair, 1, 2))

    halo_copy = remote(kv_in.at[pl.ds(0, 2)], halo, edge_sem.at[0], edge_sem.at[1], after, g)

    @pl.when(me < n - 1)
    def _():
        halo_copy.start()

    def sink_copy(dst, sem):
        return remote(sink, sink, sem, sink_rs, dst, g)

    def sink_z(zd):
        return sink_copy(at_place(zd, 0, 0), sink_zs.at[zd])

    def sink_x(xd):
        return sink_copy(at_place(z, xd, 0), sink_xs.at[xd])

    for c in local:
        c.wait()

    @pl.when(me == 0)
    def _():
        halo[...] = jnp.zeros_like(halo)
        sink[...] = kv3[0:2, :, 0:SINK]
        loop(1, nz, lambda zd: sink_z(zd).start())

    def kv_copy(block, dst, sem):
        return remote(kv_all.at[block], kv_all.at[block], sem, kv_recv.at[block], dst, g)

    def kv_wait(block):
        kv_copy(block, sib, fwd_send.at[0]).wait_recv()

    def to_z(zd):
        return kv_copy(me, at_place(zd, x, core), z_send.at[zd])

    def to_x(zs, xd):
        return kv_copy(at_place(zs, x, core), at_place(z, xd, core), x_send.at[zs, xd])

    def to_sib(at):
        return kv_copy(2 * at + core, sib, fwd_send.at[at])

    def relay(zs):
        blk = at_place(zs, lax.rem(x - turn + nx, nx), core)
        return kv_copy(blk, at_place(z, lax.rem(x + turn + nx, nx), core), relay_send.at[zs])

    def load_head(slot):
        q = q3[slot].reshape(rows, hd)
        d = do3[slot].reshape(rows, hd)
        q_r[slot] = q
        do_r[slot] = d
        q_t[slot] = q.T
        do_t[slot] = d.T
        dq_t[slot] = jnp.zeros((hd, rows), f32)

    def block(slot, acc, k, v, allowed):
        s = dot(k, q_t[slot])
        p = jnp.exp2(s * (scale * LOG2E) - aux3[slot, 0:1, :])
        if allowed is not None:
            p = jnp.where(allowed, p, 0.0)
        dp = dot(v, do_t[slot])
        ds = (p * (dp - aux3[slot, 1:2, :])).astype(bf16)
        dv = dot(p.astype(bf16), do_r[slot])
        dk = dot(ds, q_r[slot])
        dq_t[acc] += dot(k.T, ds)
        return dk * scale, dv

    def query_grads(acc):
        return (dq_t[acc] * scale).T.astype(bf16).reshape(tok, heads, hd)

    def gap(count, key_start):
        key = lax.broadcasted_iota(jnp.int32, (count, rows), 0) + key_start
        row = lax.broadcasted_iota(jnp.int32, (count, rows), 1) // heads
        return row - key

    def band(slot):
        window = windows[2 * g + slot]
        dist = gap(tok, 0)
        dk, dv = block(slot, slot, kv3[slot, 0], kv3[slot, 1], (dist >= 0) & (dist < window))
        dkv_band[slot, 0] = dk
        dkv_band[slot, 1] = dv
        if slot == 0:

            @pl.when(me > 0)
            def _():
                halo_copy.wait_recv()

        dk, dv = block(slot, slot, halo[slot, 0], halo[slot, 1], (dist < window - tok) & (me > 0))
        back_send[slot, 0] = dk.astype(bf16)
        back_send[slot, 1] = dv.astype(bf16)

    def band_sink(slot):
        sink_count = sinks[2 * g + slot]
        window = windows[2 * g + slot]
        key = lax.broadcasted_iota(jnp.int32, (SINK, rows), 0)
        dist = gap(SINK, 0)
        allowed = (key < sink_count) & (dist >= window - me * tok)
        dk, dv = block(slot, slot, sink[slot, 0], sink[slot, 1], allowed)
        sink_sum[slot, 0] = dk
        sink_sum[slot, 1] = dv
        dq_band[slot] = query_grads(slot)

    load_head(0)
    load_head(1)
    swaps[0].wait_recv()
    kv_all[me] = kv3[full_slot]
    loop(z + 1, nz, lambda zd: to_z(zd).start())
    loop(x + 1, nx, lambda xd: to_x(z, xd).start())

    @pl.when(core == 0)
    def _():
        to_sib(chip).start()

    def arrive_z(i):
        zs = z - i
        kv_wait(at_place(zs, x, core))
        if nx == 4:
            to_x(zs, lax.rem(x + 1, nx)).start()
            to_x(zs, lax.rem(x + nx - 1, nx)).start()
        else:
            for d in range(1, nx):
                to_x(zs, lax.rem(x + d, nx)).start()
        to_sib(zs * nx + x).start()

    def arrive(zs, xs):
        kv_wait(at_place(zs, xs, core))
        to_sib(zs * nx + xs).start()

    def near(zs):
        if nx == 4:
            arrive(zs, lax.rem(x - turn + nx, nx))
            relay(zs).start()
            arrive(zs, lax.rem(x + turn + nx, nx))
        else:
            for d in range(1, nx):
                arrive(zs, lax.rem(x + d, nx))

    def far(zs):
        if nx == 4:
            arrive(zs, lax.rem(x + 2, nx))

    loop(1, z + 1, arrive_z)

    @pl.when((x == 0) & (core == 0))
    def _():
        @pl.when(z > 0)
        def _():
            sink_copy(sib, sink_fs).wait_recv()

        loop(1, nx, lambda xd: sink_x(xd).start())

    band(0)
    loop(0, x, lambda xs: arrive(z, xs))
    loop(1, z + 1, lambda i: near(z - i))

    @pl.when((x > 0) & (core == 0))
    def _():
        sink_copy(sib, sink_fs).wait_recv()

    @pl.when(core == 0)
    def _():
        sink_copy(sib, sink_fs).start()

    band(1)
    loop(1, z + 1, lambda i: far(z - i))

    @pl.when(core == 1)
    def _():
        sink_copy(sib, sink_fs).wait_recv()

    band_sink(0)
    band_sink(1)

    back_copy = remote(back_send, back_recv, edge_sem.at[2], edge_sem.at[3], before, g)

    @pl.when(me > 0)
    def _():
        back_copy.start()

    def sgrad_copy(slot, dst):
        return remote(sink_send, sink_recv.at[slot], sgrad_ss, sgrad_rs.at[slot], dst, g)

    def sgrad_add(slot):
        sgrad_copy(slot, sib).wait_recv()
        sink_sum[...] += sink_recv[slot].astype(f32)

    def sgrad_send(slot, dst):
        sink_send[...] = sink_sum[...].astype(bf16)
        sgrad_copy(slot, dst).start()

    @pl.when(core == 1)
    def _():
        sgrad_send(0, sib)

    def sib_copy(dst):
        return remote(part.at[dst], sib_part, part_send.at[dst], sib_recv, sib, g)

    def spart_copy(at):
        blk = 2 * at + 1 - core
        return remote(part.at[blk], spart.at[at], part_send.at[blk], spart_recv.at[at], sib, g)

    def x_copy(zs, xs, xd):
        blk = at_place(zs, xd, core)
        return remote(
            part.at[blk], x_part.at[zs, xs], part_send.at[blk], x_recv.at[zs, xs], at_place(z, xd, core), g
        )

    def z_copy(zs, zd):
        blk = at_place(zd, x, core)
        return remote(
            part.at[blk], z_part.at[zs], part_send.at[blk], z_recv.at[zs], at_place(zd, x, core), g
        )

    def hop_copy(zs):
        blk = at_place(zs, lax.rem(x + 2, nx), core)
        to = at_place(z, lax.rem(x + turn + nx, nx), core)
        return remote(part.at[blk], hop_part.at[zs], part_send.at[blk], hop_recv.at[zs], to, g)

    def combine(at):
        zs = at // nx
        xd = lax.rem(at, nx)
        spart_copy(at).wait_recv()
        blk = 2 * at + core
        pown[at] += spart[at].astype(f32)
        straight = (zs == z) | (xd != x)
        if nx == 4:
            apart = lax.rem((xd - x) * turn + nx, nx)
            straight = (zs == z) | (apart == nx - 1)

            @pl.when((zs < z) & (apart == 2))
            def _():
                part[blk] = pown[at].astype(bf16)
                hop_copy(zs).start()

        @pl.when(straight)
        def _():
            part[blk] = pown[at].astype(bf16)
            x_copy(zs, x, xd).start()

    def hop(zs):
        if nx == 4:
            xd = lax.rem(x + turn + nx, nx)
            at = zs * nx + xd
            blk = 2 * at + core
            hop_copy(zs).wait_recv()
            part[blk] = (pown[at] + hop_part[zs].astype(f32)).astype(bf16)
            x_copy(zs, x, xd).start()

    def gather_x(zs):
        at = zs * nx + x
        blk = 2 * at + core
        for d in range(1, nx):
            if nx == 4 and d == 2:
                continue
            xs = lax.rem(x + d, nx)
            x_copy(zs, xs, x).wait_recv()
            pown[at] += x_part[zs, xs].astype(f32)
        part[blk] = pown[at].astype(bf16)
        z_copy(z, zs).start()

    for c in swaps[1:]:
        c.wait_recv()
    load_head(2)
    dk, dv = block(full_slot, 2, kv_all[me, 0], kv_all[me, 1], gap(tok, 0) >= 0)
    dkv_own[0] = dk
    dkv_own[1] = dv

    @pl.when(core == 1)
    def _():
        kv_wait(sib)
        dk, dv = block(full_slot, 2, kv_all[sib, 0], kv_all[sib, 1], None)
        part[sib, 0] = dk.astype(bf16)
        part[sib, 1] = dv.astype(bf16)
        sib_copy(sib).start()

    def step(t):
        at = chip - t
        mine = 2 * at + core
        theirs = 2 * at + 1 - core
        zs = at // nx
        kv_wait(theirs)
        dk, dv = block(full_slot, 2, kv_all[theirs, 0], kv_all[theirs, 1], None)
        part[theirs, 0] = dk.astype(bf16)
        part[theirs, 1] = dv.astype(bf16)
        spart_copy(at).start()
        dk, dv = block(full_slot, 2, kv_all[mine, 0], kv_all[mine, 1], None)
        pown[at, 0] = dk
        pown[at, 1] = dv

        @pl.when(t > 1)
        def _():
            combine(at + 1)

        @pl.when((lax.rem(at, nx) == 0) & (zs + 1 < z))
        def _():
            hop(zs + 1)

        @pl.when((lax.rem(at, nx) == 0) & (zs + 2 < z))
        def _():
            gather_x(zs + 2)

    loop(1, chip + 1, step)

    dq_full[...] = query_grads(2)
    back_q = remote(dq_full, dq_home, swap_send.at[6], swap_recv.at[6], me, pg)
    back_q.start()
    @pl.when(chip > 0)
    def _():
        combine(0)

    @pl.when(z > 0)
    def _():
        hop(0)

    @pl.when(z > 1)
    def _():
        gather_x(1)

    @pl.when(z > 0)
    def _():
        gather_x(0)

    @pl.when(core == 0)
    def _():
        sgrad_add(0)

        @pl.when(x > 0)
        def _():
            sgrad_send(x, at_place(z, 0, 0))

    @pl.when((x == 0) & (core == 0))
    def _():
        loop(1, nx, sgrad_add)

        @pl.when(z > 0)
        def _():
            sgrad_send(nx + z, 0)

    dq_near[...] = jnp.where(first_ret, dq_full[...], dq_band[0])
    out_near = pltpu.make_async_copy(dq_near, dq_out.at[:, 0], local_sem.at[0])
    out_near.start()

    @pl.when(me < n - 1)
    def _():
        back_copy.wait_recv()
        dkv_band[...] += back_recv[...].astype(f32)

    @pl.when(me == 0)
    def _():
        loop(1, nz, lambda zs: sgrad_add(nx + zs))
        dkv_band[:, :, 0:SINK] += sink_sum[...]

    @pl.when(core == 0)
    def _():
        sib_copy(me).wait_recv()
        dkv_own[...] += sib_part[...].astype(f32)

    def take_x(xs):
        x_copy(z, xs, x).wait_recv()
        dkv_own[...] += x_part[z, xs].astype(f32)

    loop(x + 1, nx, take_x)

    def take_z(zs):
        z_copy(zs, zs).wait_recv()
        dkv_own[...] += z_part[zs].astype(f32)

    loop(z + 1, nz, take_z)

    dkv_full[...] = dkv_own[...].astype(bf16)
    back_kv = remote(dkv_full, dkv_home, swap_send.at[8], swap_recv.at[8], me, pg)
    back_kv.start()
    dkv_out[0] = jnp.where(first_ret, dkv_full[...], dkv_band[0].astype(bf16))

    back_q.wait()
    dq_home[...] = jnp.where(second_ret, jnp.where(pair, dq_full[...], dq_home[...]), dq_band[1])
    out_far = pltpu.make_async_copy(dq_home, dq_out.at[:, 1], local_sem.at[1])
    out_far.start()
    back_kv.wait()
    dkv_out[1] = jnp.where(
        second_ret, jnp.where(pair, dkv_full[...], dkv_home[...]), dkv_band[1].astype(bf16)
    )

    for c in swaps:
        c.wait_send()

    loop(z + 1, nz, lambda zd: to_z(zd).wait_send())
    loop(x + 1, nx, lambda xd: to_x(z, xd).wait_send())

    def drain_z(zs):
        if nx == 4:
            to_x(zs, lax.rem(x + 1, nx)).wait_send()
            to_x(zs, lax.rem(x + nx - 1, nx)).wait_send()
            relay(zs).wait_send()
        else:
            for d in range(1, nx):
                to_x(zs, lax.rem(x + d, nx)).wait_send()

    loop(0, z, drain_z)
    loop(0, chip + 1 - core, lambda at: to_sib(at).wait_send())
    loop(0, 2 * chip + core, lambda blk: sib_copy(blk).wait_send())

    @pl.when(me < n - 1)
    def _():
        halo_copy.wait_send()

    @pl.when(me > 0)
    def _():
        back_copy.wait_send()
        sgrad_copy(0, sib).wait_send()

    @pl.when(me == 0)
    def _():
        loop(1, nz, lambda zd: sink_z(zd).wait_send())

    @pl.when((x == 0) & (core == 0))
    def _():
        loop(1, nx, lambda xd: sink_x(xd).wait_send())

    @pl.when(core == 0)
    def _():
        sink_copy(sib, sink_fs).wait_send()

    out_near.wait()
    out_far.wait()


def shards(queries, keys, values, outputs, grads, logs, kind, sinks, windows):
    tok, _, heads, hd = queries.shape
    rows = tok * heads
    n = lax.axis_size("ctx")
    nx = min(4, n // 2)
    nz = n // 2 // nx
    delta = jnp.sum(grads.astype(f32) * outputs.astype(f32), axis=-1)
    lse = logs.astype(f32) * LOG2E
    aux = jnp.stack([lse, delta], axis=0)
    aux = jnp.moveaxis(aux, 2, 0).reshape(2, 2, tok * heads)
    kv = jnp.moveaxis(jnp.stack([keys, values], axis=0), 2, 0)
    smem = pl.BlockSpec(memory_space=pltpu.SMEM)
    hbm = pl.BlockSpec(memory_space=pl.ANY)
    vmem = pl.BlockSpec(memory_space=pltpu.VMEM)
    V = pltpu.VMEM
    dma = pltpu.SemaphoreType.DMA
    dq, dkv = pl.pallas_call(
        functools.partial(kernel, n),
        in_specs=[smem, smem, smem, hbm, hbm, hbm, hbm],
        out_specs=[hbm, vmem],
        out_shape=[
            jax.ShapeDtypeStruct((tok, 2, heads, hd), bf16),
            jax.ShapeDtypeStruct((2, 2, tok, hd), bf16),
        ],
        scratch_shapes=[
            V((3, tok, heads, hd), bf16),
            V((3, tok, heads, hd), bf16),
            V((3, 2, tok, hd), bf16),
            V((3, 2, tok * heads), f32),
            V((n, 2, tok, hd), bf16),
            V((n // 2, 2, tok, hd), f32),
            V((n, 2, tok, hd), bf16),
            V((nz, nx, 2, tok, hd), bf16),
            V((nz, 2, tok, hd), bf16),
            V((nz, 2, tok, hd), bf16),
            V((2, tok, hd), bf16),
            V((n // 2, 2, tok, hd), bf16),
            V((2, 2, tok, hd), bf16),
            V((2, 2, SINK, hd), bf16),
            V((2, 2, SINK, hd), f32),
            V((2, 2, SINK, hd), bf16),
            V((nx + nz, 2, 2, SINK, hd), bf16),
            V((2, 2, tok, hd), bf16),
            V((2, 2, tok, hd), bf16),
            V((3, hd, rows), bf16),
            V((3, hd, rows), bf16),
            V((3, rows, hd), bf16),
            V((3, rows, hd), bf16),
            V((3, hd, rows), f32),
            V((2, tok, heads, hd), bf16),
            V((tok, heads, hd), bf16),
            V((tok, heads, hd), bf16),
            V((tok, heads, hd), bf16),
            V((2, tok, hd), f32),
            V((2, 2, tok, hd), f32),
            V((2, tok, hd), bf16),
            V((2, tok, hd), bf16),
            dma((12,)),
            dma((9,)),
            dma((9,)),
            dma((n,)),
            dma((nz,)),
            dma((nz, nx)),
            dma((nz,)),
            dma((n // 2,)),
            dma((n,)),
            dma((nz, nx)),
            dma((nz,)),
            dma((nz,)),
            dma,
            dma((n // 2,)),
            dma((nz,)),
            dma((nx,)),
            dma,
            dma,
            dma,
            dma((nx + nz,)),
            dma((4,)),
        ],
        compiler_params=pltpu.CompilerParams(
            collective_id=0, has_side_effects=True, vmem_limit_bytes=60 * 2**20
        ),
        name="attention_grads",
    )(kind, sinks, windows, queries, kv, grads, aux)
    dkv = jnp.moveaxis(dkv, 0, 2)
    return dq, dkv[0], dkv[1]


def solution(mesh):
    return jax.shard_map(
        shards,
        mesh=mesh,
        in_specs=(
            P("ctx", "hg", None, None),
            P("ctx", "hg", None),
            P("ctx", "hg", None),
            P("ctx", "hg", None, None),
            P("ctx", "hg", None, None),
            P("ctx", "hg", None),
            P(),
            P(),
            P(),
        ),
        out_specs=(P("ctx", "hg", None, None), P("ctx", "hg", None), P("ctx", "hg", None)),
        check_vma=False,
    )
```

```python
import functools

import jax
import jax.numpy as jnp
from jax import lax
from jax.experimental import pallas as pl
from jax.experimental.pallas import tpu as pltpu
from jax.sharding import PartitionSpec as P

SINK = 128
MESH = pl.DeviceIdType.MESH
LOG2E = 1.4426950408889634
f32 = jnp.float32
bf16 = jnp.bfloat16


def dot(a, b):
    return lax.dot_general(a, b, (((1,), (0,)), ((), ())), preferred_element_type=f32)


def kernel(
    n,
    kind,
    sinks,
    windows,
    q_in,
    kv_in,
    do_in,
    o_in,
    lse_in,
    dq_out,
    dkv_out,
    q3,
    do3,
    kv3,
    o2,
    lse3,
    delta3,
    kv_all,
    pown,
    part,
    x_part,
    hop_part,
    z_part,
    sib_part,
    spart,
    halo,
    sink,
    sink_sum,
    sink_send,
    sink_recv,
    back_send,
    back_recv,
    q_t,
    do_t,
    q_r,
    do_r,
    dq_t,
    dq_band,
    dq_full,
    dq_near,
    dq_home,
    dkv_own,
    dkv_band,
    dkv_full,
    dkv_home,
    local_sem,
    swap_send,
    swap_recv,
    kv_recv,
    z_send,
    x_send,
    relay_send,
    fwd_send,
    part_send,
    x_recv,
    hop_recv,
    z_recv,
    sib_recv,
    spart_recv,
    sink_zs,
    sink_xs,
    sink_fs,
    sink_rs,
    sgrad_ss,
    sgrad_rs,
    edge_sem,
):
    tok = kv_all.shape[2]
    heads = q_in.shape[2]
    hd = q_in.shape[3]
    rows = tok * heads
    scale = hd ** (-0.5)
    me = lax.axis_index("ctx")
    g = lax.axis_index("hg")
    pg = g + 1 - 2 * lax.rem(g, 2)
    chips = n // 2
    chip = me // 2
    core = lax.rem(me, 2)
    nx = min(4, chips)
    nz = chips // nx
    z = chip // nx
    x = lax.rem(chip, nx)
    turn = 1 - 2 * core
    sib = me + turn
    beside = lax.rem(me - turn + n, n)
    after = lax.rem(me + 1, n)
    before = lax.rem(me + n - 1, n)

    def remote(src, dst, ss, rs, ctx, hg):
        return pltpu.make_async_remote_copy(
            src_ref=src, dst_ref=dst, send_sem=ss, recv_sem=rs, device_id=(ctx, hg), device_id_type=MESH
        )

    def at_place(pz, px, pc):
        return (pz * nx + px) * 2 + pc

    def loop(lo, hi, body):
        def one(i, _):
            body(i)
            return 0

        lax.fori_loop(lo, hi, one, 0)

    local = []
    for slot in range(2):
        local.append((kv_in.at[slot], kv3.at[slot]))
        local.append((q_in.at[:, slot], q3.at[slot]))
        local.append((do_in.at[:, slot], do3.at[slot]))
        local.append((o_in.at[:, slot], o2.at[slot]))
        local.append((lse_in.at[slot], lse3.at[slot]))
    local = [pltpu.make_async_copy(a, b, local_sem.at[i]) for i, (a, b) in enumerate(local)]
    for c in local:
        c.start()

    barrier = pltpu.get_barrier_semaphore()

    def greet(ctx, hg):
        pl.semaphore_signal(barrier, inc=1, device_id=(ctx, hg), device_id_type=MESH)

    greet(me, pg)
    greet(sib, g)
    greet(beside, g)
    for d in range(1, nz):
        greet(at_place(lax.rem(z + d, nz), x, core), g)
    for d in range(1, nx):
        greet(at_place(z, lax.rem(x + d, nx), core), g)
    pl.semaphore_wait(barrier, 1 + nz + nx)

    pieces = [
        (kv_in.at[1], kv3.at[2]),
        (lse_in.at[1], lse3.at[2]),
        (q_in.at[:, 1], q3.at[2]),
        (do_in.at[:, 1], do3.at[2]),
    ]
    swaps = [remote(a, b, swap_send.at[i], swap_recv.at[i], me, pg) for i, (a, b) in enumerate(pieces)]
    for c in swaps:
        c.start()

    kinds = [kind[2 * g], kind[2 * g + 1]]
    first_ret = kinds[0] == 1
    second_ret = kinds[1] == 1
    pair = kinds[0] + kinds[1] == 1
    full_slot = jnp.where(first_ret, 0, jnp.where(pair, 1, 2))

    halo_copy = remote(kv_in.at[pl.ds(0, 2)], halo, edge_sem.at[0], edge_sem.at[1], after, g)

    @pl.when(me < n - 1)
    def _():
        halo_copy.start()

    def sink_copy(dst, sem):
        return remote(sink, sink, sem, sink_rs, dst, g)

    def sink_z(zd):
        return sink_copy(at_place(zd, 0, 0), sink_zs.at[zd])

    def sink_x(xd):
        return sink_copy(at_place(z, xd, 0), sink_xs.at[xd])

    for c in local:
        c.wait()

    @pl.when(me == 0)
    def _():
        halo[...] = jnp.zeros_like(halo)
        sink[...] = kv3[0:2, :, 0:SINK]
        loop(1, nz, lambda zd: sink_z(zd).start())

    def kv_copy(block, dst, sem):
        return remote(kv_all.at[block], kv_all.at[block], sem, kv_recv.at[block], dst, g)

    def kv_wait(block):
        kv_copy(block, sib, fwd_send.at[0]).wait_recv()

    def to_z(zd):
        return kv_copy(me, at_place(zd, x, core), z_send.at[zd])

    def to_x(zs, xd):
        return kv_copy(at_place(zs, x, core), at_place(z, xd, core), x_send.at[zs, xd])

    def to_sib(at):
        return kv_copy(2 * at + core, sib, fwd_send.at[at])

    def relay(zs):
        blk = at_place(zs, lax.rem(x - turn + nx, nx), core)
        return kv_copy(blk, at_place(z, lax.rem(x + turn + nx, nx), core), relay_send.at[zs])

    def load_head(slot):
        q = q3[slot].reshape(rows, hd)
        d = do3[slot].reshape(rows, hd)
        q_r[slot] = q
        do_r[slot] = d
        q_t[slot] = q.T
        do_t[slot] = d.T
        dq_t[slot] = jnp.zeros((hd, rows), f32)

    def row_totals(slot):
        o_t = o2[slot].reshape(rows, hd).T.astype(f32)
        delta3[slot] = jnp.sum(o_t * do_t[slot].astype(f32), axis=0, keepdims=True)

    def block(slot, acc, k, v, allowed):
        s = dot(k, q_t[slot])
        p = jnp.exp2(s * (scale * LOG2E) - lse3[slot])
        if allowed is not None:
            p = jnp.where(allowed, p, 0.0)
        dp = dot(v, do_t[slot])
        ds = (p * (dp - delta3[slot])).astype(bf16)
        dv = dot(p.astype(bf16), do_r[slot])
        dk = dot(ds, q_r[slot])
        dq_t[acc] += dot(k.T, ds)
        return dk * scale, dv

    def query_grads(acc):
        return (dq_t[acc] * scale).T.astype(bf16).reshape(tok, heads, hd)

    def gap(count, key_start):
        key = lax.broadcasted_iota(jnp.int32, (count, rows), 0) + key_start
        row = lax.broadcasted_iota(jnp.int32, (count, rows), 1) // heads
        return row - key

    def band(slot):
        window = windows[2 * g + slot]
        dist = gap(tok, 0)
        dk, dv = block(slot, slot, kv3[slot, 0], kv3[slot, 1], (dist >= 0) & (dist < window))
        dkv_band[slot, 0] = dk
        dkv_band[slot, 1] = dv
        if slot == 0:

            @pl.when(me > 0)
            def _():
                halo_copy.wait_recv()

        dk, dv = block(slot, slot, halo[slot, 0], halo[slot, 1], (dist < window - tok) & (me > 0))
        back_send[slot, 0] = dk.astype(bf16)
        back_send[slot, 1] = dv.astype(bf16)

    def band_sink(slot):
        sink_count = sinks[2 * g + slot]
        window = windows[2 * g + slot]
        key = lax.broadcasted_iota(jnp.int32, (SINK, rows), 0)
        dist = gap(SINK, 0)
        allowed = (key < sink_count) & (dist >= window - me * tok)
        dk, dv = block(slot, slot, sink[slot, 0], sink[slot, 1], allowed)
        sink_sum[slot, 0] = dk
        sink_sum[slot, 1] = dv
        dq_band[slot] = query_grads(slot)

    load_head(1)
    row_totals(1)
    delta_copy = remote(delta3.at[1], delta3.at[2], swap_send.at[4], swap_recv.at[4], me, pg)
    delta_copy.start()
    load_head(0)
    row_totals(0)
    swaps[0].wait_recv()
    kv_all[me] = kv3[full_slot]
    loop(z + 1, nz, lambda zd: to_z(zd).start())
    loop(x + 1, nx, lambda xd: to_x(z, xd).start())

    @pl.when(core == 0)
    def _():
        to_sib(chip).start()

    def arrive_z(i):
        zs = z - i
        kv_wait(at_place(zs, x, core))
        if nx == 4:
            to_x(zs, lax.rem(x + 1, nx)).start()
            to_x(zs, lax.rem(x + nx - 1, nx)).start()
        else:
            for d in range(1, nx):
                to_x(zs, lax.rem(x + d, nx)).start()
        to_sib(zs * nx + x).start()

    def arrive(zs, xs):
        kv_wait(at_place(zs, xs, core))
        to_sib(zs * nx + xs).start()

    def near(zs):
        if nx == 4:
            arrive(zs, lax.rem(x - turn + nx, nx))
            relay(zs).start()
            arrive(zs, lax.rem(x + turn + nx, nx))
        else:
            for d in range(1, nx):
                arrive(zs, lax.rem(x + d, nx))

    def far(zs):
        if nx == 4:
            arrive(zs, lax.rem(x + 2, nx))

    @pl.when((x == 0) & (core == 0))
    def _():
        @pl.when(z > 0)
        def _():
            sink_copy(sib, sink_fs).wait_recv()

        loop(1, nx, lambda xd: sink_x(xd).start())

    loop(1, z + 1, arrive_z)

    @pl.when((x > 0) & (core == 0))
    def _():
        sink_copy(sib, sink_fs).wait_recv()

    @pl.when(core == 0)
    def _():
        sink_copy(sib, sink_fs).start()

    band(0)
    loop(0, x, lambda xs: arrive(z, xs))
    band(1)
    loop(1, z + 1, lambda i: near(z - i))

    @pl.when(core == 1)
    def _():
        sink_copy(sib, sink_fs).wait_recv()

    band_sink(0)
    band_sink(1)
    loop(1, z + 1, lambda i: far(z - i))

    back_copy = remote(back_send, back_recv, edge_sem.at[2], edge_sem.at[3], before, g)

    @pl.when(me > 0)
    def _():
        back_copy.start()

    def sgrad_copy(slot, dst):
        return remote(sink_send, sink_recv.at[slot], sgrad_ss, sgrad_rs.at[slot], dst, g)

    def sgrad_add(slot):
        sgrad_copy(slot, sib).wait_recv()
        sink_sum[...] += sink_recv[slot].astype(f32)

    def sgrad_send(slot, dst):
        sink_send[...] = sink_sum[...].astype(bf16)
        sgrad_copy(slot, dst).start()

    @pl.when(core == 1)
    def _():
        sgrad_send(0, sib)

    def sib_copy(dst):
        return remote(part.at[dst], sib_part, part_send.at[dst], sib_recv, sib, g)

    def spart_copy(at):
        blk = 2 * at + 1 - core
        return remote(part.at[blk], spart.at[at], part_send.at[blk], spart_recv.at[at], sib, g)

    def x_copy(zs, xs, xd):
        blk = at_place(zs, xd, core)
        return remote(
            part.at[blk], x_part.at[zs, xs], part_send.at[blk], x_recv.at[zs, xs], at_place(z, xd, core), g
        )

    def z_copy(zs, zd):
        blk = at_place(zd, x, core)
        return remote(
            part.at[blk], z_part.at[zs], part_send.at[blk], z_recv.at[zs], at_place(zd, x, core), g
        )

    def hop_copy(zs):
        blk = at_place(zs, lax.rem(x + 2, nx), core)
        to = at_place(z, lax.rem(x + turn + nx, nx), core)
        return remote(part.at[blk], hop_part.at[zs], part_send.at[blk], hop_recv.at[zs], to, g)

    def combine(at):
        zs = at // nx
        xd = lax.rem(at, nx)
        spart_copy(at).wait_recv()
        blk = 2 * at + core
        pown[at] += spart[at].astype(f32)
        straight = (zs == z) | (xd != x)
        if nx == 4:
            apart = lax.rem((xd - x) * turn + nx, nx)
            straight = (zs == z) | (apart == nx - 1)

            @pl.when((zs < z) & (apart == 2))
            def _():
                part[blk] = pown[at].astype(bf16)
                hop_copy(zs).start()

        @pl.when(straight)
        def _():
            part[blk] = pown[at].astype(bf16)
            x_copy(zs, x, xd).start()

    def hop(zs):
        if nx == 4:
            xd = lax.rem(x + turn + nx, nx)
            at = zs * nx + xd
            blk = 2 * at + core
            hop_copy(zs).wait_recv()
            part[blk] = (pown[at] + hop_part[zs].astype(f32)).astype(bf16)
            x_copy(zs, x, xd).start()

    def gather_x(zs):
        at = zs * nx + x
        blk = 2 * at + core
        for d in range(1, nx):
            if nx == 4 and d == 2:
                continue
            xs = lax.rem(x + d, nx)
            x_copy(zs, xs, x).wait_recv()
            pown[at] += x_part[zs, xs].astype(f32)
        part[blk] = pown[at].astype(bf16)
        z_copy(z, zs).start()

    for c in swaps[1:]:
        c.wait_recv()
    delta_copy.wait_recv()
    load_head(2)
    def step(at):
        mine = 2 * at + core
        theirs = 2 * at + 1 - core
        zs = at // nx
        kv_wait(theirs)
        dk, dv = block(full_slot, 2, kv_all[theirs, 0], kv_all[theirs, 1], None)
        part[theirs, 0] = dk.astype(bf16)
        part[theirs, 1] = dv.astype(bf16)
        spart_copy(at).start()
        dk, dv = block(full_slot, 2, kv_all[mine, 0], kv_all[mine, 1], None)
        pown[at, 0] = dk
        pown[at, 1] = dv

        @pl.when(at > 0)
        def _():
            combine(at - 1)

        @pl.when((lax.rem(at, nx) == 0) & (zs > 0))
        def _():
            hop(zs - 1)

        @pl.when((lax.rem(at, nx) == 0) & (zs > 1))
        def _():
            gather_x(zs - 2)

    loop(0, chip, step)

    @pl.when(core == 1)
    def _():
        kv_wait(sib)
        dk, dv = block(full_slot, 2, kv_all[sib, 0], kv_all[sib, 1], None)
        part[sib, 0] = dk.astype(bf16)
        part[sib, 1] = dv.astype(bf16)
        sib_copy(sib).start()

    @pl.when(chip > 0)
    def _():
        combine(chip - 1)

    @pl.when((z > 0) & (x == 0))
    def _():
        hop(z - 1)

    @pl.when((z > 1) & (x == 0))
    def _():
        gather_x(z - 2)

    @pl.when(z > 0)
    def _():
        gather_x(z - 1)

    dk, dv = block(full_slot, 2, kv_all[me, 0], kv_all[me, 1], gap(tok, 0) >= 0)
    dkv_own[0] = dk
    dkv_own[1] = dv


    back_q = []
    for i in range(2):
        here = pl.ds(i * (tok // 2), tok // 2)
        grads = dq_t[2, :, i * (rows // 2) : (i + 1) * (rows // 2)] * scale
        dq_full[here] = grads.T.astype(bf16).reshape(tok // 2, heads, hd)
        c = remote(dq_full.at[here], dq_home.at[here], swap_send.at[5 + i], swap_recv.at[5 + i], me, pg)
        c.start()
        back_q.append(c)

    @pl.when(core == 0)
    def _():
        sgrad_add(0)

        @pl.when(x > 0)
        def _():
            sgrad_send(x, at_place(z, 0, 0))

    @pl.when((x == 0) & (core == 0))
    def _():
        loop(1, nx, sgrad_add)

        @pl.when(z > 0)
        def _():
            sgrad_send(nx + z, 0)

    dq_near[...] = jnp.where(first_ret, dq_full[...], dq_band[0])
    out_near = pltpu.make_async_copy(dq_near, dq_out.at[:, 0], local_sem.at[0])
    out_near.start()

    @pl.when(me < n - 1)
    def _():
        back_copy.wait_recv()
        dkv_band[...] += back_recv[...].astype(f32)

    @pl.when(me == 0)
    def _():
        loop(1, nz, lambda zs: sgrad_add(nx + zs))
        dkv_band[:, :, 0:SINK] += sink_sum[...]

    @pl.when(core == 0)
    def _():
        sib_copy(me).wait_recv()
        dkv_own[...] += sib_part[...].astype(f32)

    def take_x(xs):
        x_copy(z, xs, x).wait_recv()
        dkv_own[...] += x_part[z, xs].astype(f32)

    loop(x + 1, nx, take_x)

    def take_z(zs):
        z_copy(zs, zs).wait_recv()
        dkv_own[...] += z_part[zs].astype(f32)

    loop(z + 1, nz, take_z)

    dkv_full[...] = dkv_own[...].astype(bf16)
    back_kv = remote(dkv_full, dkv_home, swap_send.at[8], swap_recv.at[8], me, pg)
    back_kv.start()
    dkv_out[0] = jnp.where(first_ret, dkv_full[...], dkv_band[0].astype(bf16))

    out_far = []
    for i in range(2):
        here = pl.ds(i * (tok // 2), tok // 2)
        back_q[i].wait()
        home = jnp.where(pair, dq_full[here], dq_home[here])
        dq_home[here] = jnp.where(second_ret, home, dq_band[1, here])
        c = pltpu.make_async_copy(dq_home.at[here], dq_out.at[here, 1], local_sem.at[1 + i])
        c.start()
        out_far.append(c)
    back_kv.wait()
    dkv_out[1] = jnp.where(
        second_ret, jnp.where(pair, dkv_full[...], dkv_home[...]), dkv_band[1].astype(bf16)
    )

    for c in swaps:
        c.wait_send()
    delta_copy.wait_send()

    loop(z + 1, nz, lambda zd: to_z(zd).wait_send())
    loop(x + 1, nx, lambda xd: to_x(z, xd).wait_send())

    def drain_z(zs):
        if nx == 4:
            to_x(zs, lax.rem(x + 1, nx)).wait_send()
            to_x(zs, lax.rem(x + nx - 1, nx)).wait_send()
            relay(zs).wait_send()
        else:
            for d in range(1, nx):
                to_x(zs, lax.rem(x + d, nx)).wait_send()

    loop(0, z, drain_z)
    loop(0, chip + 1 - core, lambda at: to_sib(at).wait_send())
    loop(0, 2 * chip + core, lambda blk: sib_copy(blk).wait_send())

    @pl.when(me < n - 1)
    def _():
        halo_copy.wait_send()

    @pl.when(me > 0)
    def _():
        back_copy.wait_send()
        sgrad_copy(0, sib).wait_send()

    @pl.when(me == 0)
    def _():
        loop(1, nz, lambda zd: sink_z(zd).wait_send())

    @pl.when((x == 0) & (core == 0))
    def _():
        loop(1, nx, lambda xd: sink_x(xd).wait_send())

    @pl.when(core == 0)
    def _():
        sink_copy(sib, sink_fs).wait_send()

    out_near.wait()
    for c in out_far:
        c.wait()


def shards(queries, keys, values, outputs, grads, logs, kind, sinks, windows):
    tok, _, heads, hd = queries.shape
    rows = tok * heads
    n = lax.axis_size("ctx")
    nx = min(4, n // 2)
    nz = n // 2 // nx
    lse = jnp.moveaxis(logs.astype(f32) * LOG2E, 1, 0).reshape(2, 1, rows)
    kv = jnp.moveaxis(jnp.stack([keys, values], axis=0), 2, 0)
    smem = pl.BlockSpec(memory_space=pltpu.SMEM)
    hbm = pl.BlockSpec(memory_space=pl.ANY)
    vmem = pl.BlockSpec(memory_space=pltpu.VMEM)
    V = pltpu.VMEM
    dma = pltpu.SemaphoreType.DMA
    dq, dkv = pl.pallas_call(
        functools.partial(kernel, n),
        in_specs=[smem, smem, smem, hbm, hbm, hbm, hbm, hbm],
        out_specs=[hbm, vmem],
        out_shape=[
            jax.ShapeDtypeStruct((tok, 2, heads, hd), bf16),
            jax.ShapeDtypeStruct((2, 2, tok, hd), bf16),
        ],
        scratch_shapes=[
            V((3, tok, heads, hd), bf16),
            V((3, tok, heads, hd), bf16),
            V((3, 2, tok, hd), bf16),
            V((2, tok, heads, hd), bf16),
            V((3, 1, rows), f32),
            V((3, 1, rows), f32),
            V((n, 2, tok, hd), bf16),
            V((n // 2, 2, tok, hd), f32),
            V((n, 2, tok, hd), bf16),
            V((nz, nx, 2, tok, hd), bf16),
            V((nz, 2, tok, hd), bf16),
            V((nz, 2, tok, hd), bf16),
            V((2, tok, hd), bf16),
            V((n // 2, 2, tok, hd), bf16),
            V((2, 2, tok, hd), bf16),
            V((2, 2, SINK, hd), bf16),
            V((2, 2, SINK, hd), f32),
            V((2, 2, SINK, hd), bf16),
            V((nx + nz, 2, 2, SINK, hd), bf16),
            V((2, 2, tok, hd), bf16),
            V((2, 2, tok, hd), bf16),
            V((3, hd, rows), bf16),
            V((3, hd, rows), bf16),
            V((3, rows, hd), bf16),
            V((3, rows, hd), bf16),
            V((3, hd, rows), f32),
            V((2, tok, heads, hd), bf16),
            V((tok, heads, hd), bf16),
            V((tok, heads, hd), bf16),
            V((tok, heads, hd), bf16),
            V((2, tok, hd), f32),
            V((2, 2, tok, hd), f32),
            V((2, tok, hd), bf16),
            V((2, tok, hd), bf16),
            dma((10,)),
            dma((9,)),
            dma((9,)),
            dma((n,)),
            dma((nz,)),
            dma((nz, nx)),
            dma((nz,)),
            dma((n // 2,)),
            dma((n,)),
            dma((nz, nx)),
            dma((nz,)),
            dma((nz,)),
            dma,
            dma((n // 2,)),
            dma((nz,)),
            dma((nx,)),
            dma,
            dma,
            dma,
            dma((nx + nz,)),
            dma((4,)),
        ],
        compiler_params=pltpu.CompilerParams(
            collective_id=0, has_side_effects=True, vmem_limit_bytes=60 * 2**20
        ),
        name="attention_grads",
    )(kind, sinks, windows, queries, kv, grads, outputs, lse)
    dkv = jnp.moveaxis(dkv, 0, 2)
    return dq, dkv[0], dkv[1]


def solution(mesh):
    return jax.shard_map(
        shards,
        mesh=mesh,
        in_specs=(
            P("ctx", "hg", None, None),
            P("ctx", "hg", None),
            P("ctx", "hg", None),
            P("ctx", "hg", None, None),
            P("ctx", "hg", None, None),
            P("ctx", "hg", None),
            P(),
            P(),
            P(),
        ),
        out_specs=(P("ctx", "hg", None, None), P("ctx", "hg", None), P("ctx", "hg", None)),
        check_vma=False,
    )
```

```python
import functools

import jax
import jax.numpy as jnp
from jax import lax
from jax.experimental import pallas as pl
from jax.experimental.pallas import tpu as pltpu
from jax.sharding import PartitionSpec as P

SINK = 128
MESH = pl.DeviceIdType.MESH
LOG2E = 1.4426950408889634
f32 = jnp.float32
bf16 = jnp.bfloat16


def dot(a, b):
    return lax.dot_general(a, b, (((1,), (0,)), ((), ())), preferred_element_type=f32)


def kernel(
    n,
    kind,
    sinks,
    windows,
    q_in,
    kv_in,
    do_in,
    o_in,
    lse_in,
    dq_out,
    dkv_out,
    q3,
    do3,
    kv3,
    o2,
    lse3,
    delta3,
    kv_all,
    pown,
    part,
    x_part,
    hop_part,
    z_part,
    sib_part,
    spart,
    halo,
    sink,
    sink_sum,
    sink_send,
    sink_recv,
    back_send,
    back_recv,
    q_t,
    do_t,
    q_r,
    do_r,
    dq_t,
    dq_band,
    dq_full,
    dq_near,
    dq_home,
    dkv_own,
    dkv_band,
    dkv_full,
    dkv_home,
    local_sem,
    swap_send,
    swap_recv,
    kv_recv,
    z_send,
    x_send,
    relay_send,
    fwd_send,
    part_send,
    x_recv,
    hop_recv,
    z_recv,
    sib_recv,
    spart_recv,
    sink_zs,
    sink_xs,
    sink_fs,
    sink_rs,
    sgrad_ss,
    sgrad_rs,
    edge_sem,
):
    tok = kv_all.shape[2]
    heads = q_in.shape[2]
    hd = q_in.shape[3]
    rows = tok * heads
    scale = hd ** (-0.5)
    me = lax.axis_index("ctx")
    g = lax.axis_index("hg")
    pg = g + 1 - 2 * lax.rem(g, 2)
    chips = n // 2
    chip = me // 2
    core = lax.rem(me, 2)
    nx = min(4, chips)
    nz = chips // nx
    z = chip // nx
    x = lax.rem(chip, nx)
    turn = 1 - 2 * core
    sib = me + turn
    beside = lax.rem(me - turn + n, n)
    after = lax.rem(me + 1, n)
    before = lax.rem(me + n - 1, n)

    def remote(src, dst, ss, rs, ctx, hg):
        return pltpu.make_async_remote_copy(
            src_ref=src, dst_ref=dst, send_sem=ss, recv_sem=rs, device_id=(ctx, hg), device_id_type=MESH
        )

    def at_place(pz, px, pc):
        return (pz * nx + px) * 2 + pc

    def loop(lo, hi, body):
        def one(i, _):
            body(i)
            return 0

        lax.fori_loop(lo, hi, one, 0)

    local = []
    for slot in range(2):
        local.append((kv_in.at[slot], kv3.at[slot]))
        local.append((q_in.at[:, slot], q3.at[slot]))
        local.append((do_in.at[:, slot], do3.at[slot]))
        local.append((o_in.at[:, slot], o2.at[slot]))
        local.append((lse_in.at[slot], lse3.at[slot]))
    local = [pltpu.make_async_copy(a, b, local_sem.at[i]) for i, (a, b) in enumerate(local)]
    for c in local:
        c.start()

    barrier = pltpu.get_barrier_semaphore()

    def greet(ctx, hg):
        pl.semaphore_signal(barrier, inc=1, device_id=(ctx, hg), device_id_type=MESH)

    greet(me, pg)
    greet(sib, g)
    greet(beside, g)
    for d in range(1, nz):
        greet(at_place(lax.rem(z + d, nz), x, core), g)
    for d in range(1, nx):
        greet(at_place(z, lax.rem(x + d, nx), core), g)
    pl.semaphore_wait(barrier, 1 + nz + nx)

    pieces = [
        (kv_in.at[1], kv3.at[2]),
        (lse_in.at[1], lse3.at[2]),
        (q_in.at[:, 1], q3.at[2]),
        (do_in.at[:, 1], do3.at[2]),
    ]
    swaps = [remote(a, b, swap_send.at[i], swap_recv.at[i], me, pg) for i, (a, b) in enumerate(pieces)]
    swaps[0].start()

    kinds = [kind[2 * g], kind[2 * g + 1]]
    first_ret = kinds[0] == 1
    second_ret = kinds[1] == 1
    pair = kinds[0] + kinds[1] == 1
    full_slot = jnp.where(first_ret, 0, jnp.where(pair, 1, 2))

    halo_copy = remote(kv_in.at[pl.ds(0, 2)], halo, edge_sem.at[0], edge_sem.at[1], after, g)

    @pl.when(me < n - 1)
    def _():
        halo_copy.start()

    def sink_copy(dst, sem):
        return remote(sink, sink, sem, sink_rs, dst, g)

    def sink_z(zd):
        return sink_copy(at_place(zd, 0, 0), sink_zs.at[zd])

    def sink_x(xd):
        return sink_copy(at_place(z, xd, 0), sink_xs.at[xd])

    for c in local:
        c.wait()

    @pl.when(me == 0)
    def _():
        halo[...] = jnp.zeros_like(halo)
        sink[...] = kv3[0:2, :, 0:SINK]
        loop(1, nz, lambda zd: sink_z(zd).start())

    def kv_copy(block, dst, sem):
        return remote(kv_all.at[block], kv_all.at[block], sem, kv_recv.at[block], dst, g)

    def kv_wait(block):
        kv_copy(block, sib, fwd_send.at[0]).wait_recv()

    def to_z(zd):
        return kv_copy(me, at_place(zd, x, core), z_send.at[zd])

    def to_x(zs, xd):
        return kv_copy(at_place(zs, x, core), at_place(z, xd, core), x_send.at[zs, xd])

    def to_sib(at):
        return kv_copy(2 * at + core, sib, fwd_send.at[at])

    def relay(zs):
        blk = at_place(zs, lax.rem(x - turn + nx, nx), core)
        return kv_copy(blk, at_place(z, lax.rem(x + turn + nx, nx), core), relay_send.at[zs])

    def load_head(slot):
        q = q3[slot].reshape(rows, hd)
        d = do3[slot].reshape(rows, hd)
        q_r[slot] = q
        do_r[slot] = d
        q_t[slot] = q.T
        do_t[slot] = d.T
        dq_t[slot] = jnp.zeros((hd, rows), f32)

    def row_totals(slot):
        o_t = o2[slot].reshape(rows, hd).T.astype(f32)
        delta3[slot] = jnp.sum(o_t * do_t[slot].astype(f32), axis=0, keepdims=True)

    def block(slot, acc, k, v, allowed):
        s = dot(k, q_t[slot])
        p = jnp.exp2(s * (scale * LOG2E) - lse3[slot])
        if allowed is not None:
            p = jnp.where(allowed, p, 0.0)
        dp = dot(v, do_t[slot])
        ds = (p * (dp - delta3[slot])).astype(bf16)
        dv = dot(p.astype(bf16), do_r[slot])
        dk = dot(ds, q_r[slot])
        dq_t[acc] += dot(k.T, ds)
        return dk * scale, dv

    def query_grads(acc):
        return (dq_t[acc] * scale).T.astype(bf16).reshape(tok, heads, hd)

    def gap(count, key_start):
        key = lax.broadcasted_iota(jnp.int32, (count, rows), 0) + key_start
        row = lax.broadcasted_iota(jnp.int32, (count, rows), 1) // heads
        return row - key

    def band(slot):
        window = windows[2 * g + slot]
        dist = gap(tok, 0)
        dk, dv = block(slot, slot, kv3[slot, 0], kv3[slot, 1], (dist >= 0) & (dist < window))
        dkv_band[slot, 0] = dk
        dkv_band[slot, 1] = dv
        if slot == 0:

            @pl.when(me > 0)
            def _():
                halo_copy.wait_recv()

        dk, dv = block(slot, slot, halo[slot, 0], halo[slot, 1], (dist < window - tok) & (me > 0))
        back_send[slot, 0] = dk.astype(bf16)
        back_send[slot, 1] = dv.astype(bf16)

    def band_sink(slot):
        sink_count = sinks[2 * g + slot]
        window = windows[2 * g + slot]
        key = lax.broadcasted_iota(jnp.int32, (SINK, rows), 0)
        dist = gap(SINK, 0)
        allowed = (key < sink_count) & (dist >= window - me * tok)
        dk, dv = block(slot, slot, sink[slot, 0], sink[slot, 1], allowed)
        sink_sum[slot, 0] = dk
        sink_sum[slot, 1] = dv
        dq_band[slot] = query_grads(slot)

    load_head(1)
    row_totals(1)
    delta_copy = remote(delta3.at[1], delta3.at[2], swap_send.at[4], swap_recv.at[4], me, pg)
    delta_copy.start()
    load_head(0)
    row_totals(0)
    swaps[0].wait_recv()
    for c in swaps[1:]:
        c.start()
    kv_all[me] = kv3[full_slot]
    loop(z + 1, nz, lambda zd: to_z(zd).start())
    loop(x + 1, nx, lambda xd: to_x(z, xd).start())

    @pl.when(core == 0)
    def _():
        to_sib(chip).start()

    def arrive_z(i):
        zs = z - i
        kv_wait(at_place(zs, x, core))
        if nx == 4:
            to_x(zs, lax.rem(x + 1, nx)).start()
            to_x(zs, lax.rem(x + nx - 1, nx)).start()
        else:
            for d in range(1, nx):
                to_x(zs, lax.rem(x + d, nx)).start()
        to_sib(zs * nx + x).start()

    def arrive(zs, xs):
        kv_wait(at_place(zs, xs, core))
        to_sib(zs * nx + xs).start()

    def near(zs):
        if nx == 4:
            arrive(zs, lax.rem(x - turn + nx, nx))
            relay(zs).start()
            arrive(zs, lax.rem(x + turn + nx, nx))
        else:
            for d in range(1, nx):
                arrive(zs, lax.rem(x + d, nx))

    def far(zs):
        if nx == 4:
            arrive(zs, lax.rem(x + 2, nx))

    @pl.when((x == 0) & (core == 0))
    def _():
        @pl.when(z > 0)
        def _():
            sink_copy(sib, sink_fs).wait_recv()

        loop(1, nx, lambda xd: sink_x(xd).start())

    loop(1, z + 1, arrive_z)

    @pl.when((x > 0) & (core == 0))
    def _():
        sink_copy(sib, sink_fs).wait_recv()

    @pl.when(core == 0)
    def _():
        sink_copy(sib, sink_fs).start()

    band(0)
    loop(0, x, lambda xs: arrive(z, xs))
    loop(1, z + 1, lambda i: near(z - i))
    band(1)
    loop(1, z + 1, lambda i: far(z - i))

    @pl.when(core == 1)
    def _():
        sink_copy(sib, sink_fs).wait_recv()

    band_sink(0)
    band_sink(1)

    back_copy = remote(back_send, back_recv, edge_sem.at[2], edge_sem.at[3], before, g)

    @pl.when(me > 0)
    def _():
        back_copy.start()

    def sgrad_copy(slot, dst):
        return remote(sink_send, sink_recv.at[slot], sgrad_ss, sgrad_rs.at[slot], dst, g)

    def sgrad_add(slot):
        sgrad_copy(slot, sib).wait_recv()
        sink_sum[...] += sink_recv[slot].astype(f32)

    def sgrad_send(slot, dst):
        sink_send[...] = sink_sum[...].astype(bf16)
        sgrad_copy(slot, dst).start()

    @pl.when(core == 1)
    def _():
        sgrad_send(0, sib)

    def sib_copy(dst):
        return remote(part.at[dst], sib_part, part_send.at[dst], sib_recv, sib, g)

    def spart_copy(at):
        blk = 2 * at + 1 - core
        return remote(part.at[blk], spart.at[at], part_send.at[blk], spart_recv.at[at], sib, g)

    def x_copy(zs, xs, xd):
        blk = at_place(zs, xd, core)
        return remote(
            part.at[blk], x_part.at[zs, xs], part_send.at[blk], x_recv.at[zs, xs], at_place(z, xd, core), g
        )

    def z_copy(zs, zd):
        blk = at_place(zd, x, core)
        return remote(
            part.at[blk], z_part.at[zs], part_send.at[blk], z_recv.at[zs], at_place(zd, x, core), g
        )

    def hop_copy(zs):
        blk = at_place(zs, lax.rem(x + 2, nx), core)
        to = at_place(z, lax.rem(x + turn + nx, nx), core)
        return remote(part.at[blk], hop_part.at[zs], part_send.at[blk], hop_recv.at[zs], to, g)

    def combine(at):
        zs = at // nx
        xd = lax.rem(at, nx)
        spart_copy(at).wait_recv()
        blk = 2 * at + core
        pown[at] += spart[at].astype(f32)
        straight = (zs == z) | (xd != x)
        if nx == 4:
            apart = lax.rem((xd - x) * turn + nx, nx)
            straight = (zs == z) | (apart == nx - 1)

            @pl.when((zs < z) & (apart == 2))
            def _():
                part[blk] = pown[at].astype(bf16)
                hop_copy(zs).start()

        @pl.when(straight)
        def _():
            part[blk] = pown[at].astype(bf16)
            x_copy(zs, x, xd).start()

    def hop(zs):
        if nx == 4:
            xd = lax.rem(x + turn + nx, nx)
            at = zs * nx + xd
            blk = 2 * at + core
            hop_copy(zs).wait_recv()
            part[blk] = (pown[at] + hop_part[zs].astype(f32)).astype(bf16)
            x_copy(zs, x, xd).start()

    def gather_x(zs):
        at = zs * nx + x
        blk = 2 * at + core
        for d in range(1, nx):
            if nx == 4 and d == 2:
                continue
            xs = lax.rem(x + d, nx)
            x_copy(zs, xs, x).wait_recv()
            pown[at] += x_part[zs, xs].astype(f32)
        part[blk] = pown[at].astype(bf16)
        z_copy(z, zs).start()

    for c in swaps[1:]:
        c.wait_recv()
    delta_copy.wait_recv()
    load_head(2)
    def step(at):
        mine = 2 * at + core
        theirs = 2 * at + 1 - core
        zs = at // nx
        kv_wait(theirs)
        dk, dv = block(full_slot, 2, kv_all[theirs, 0], kv_all[theirs, 1], None)
        part[theirs, 0] = dk.astype(bf16)
        part[theirs, 1] = dv.astype(bf16)
        spart_copy(at).start()
        dk, dv = block(full_slot, 2, kv_all[mine, 0], kv_all[mine, 1], None)
        pown[at, 0] = dk
        pown[at, 1] = dv

        @pl.when(at > 0)
        def _():
            combine(at - 1)

        @pl.when((lax.rem(at, nx) == 0) & (zs > 0))
        def _():
            hop(zs - 1)

        @pl.when((lax.rem(at, nx) == 0) & (zs > 1))
        def _():
            gather_x(zs - 2)

    loop(0, chip, step)

    @pl.when(core == 1)
    def _():
        kv_wait(sib)
        dk, dv = block(full_slot, 2, kv_all[sib, 0], kv_all[sib, 1], None)
        part[sib, 0] = dk.astype(bf16)
        part[sib, 1] = dv.astype(bf16)
        sib_copy(sib).start()

    @pl.when(chip > 0)
    def _():
        combine(chip - 1)

    @pl.when((z > 0) & (x == 0))
    def _():
        hop(z - 1)

    @pl.when((z > 1) & (x == 0))
    def _():
        gather_x(z - 2)

    @pl.when(z > 0)
    def _():
        gather_x(z - 1)

    dk, dv = block(full_slot, 2, kv_all[me, 0], kv_all[me, 1], gap(tok, 0) >= 0)
    dkv_own[0] = dk
    dkv_own[1] = dv


    back_q = []
    for i in range(2):
        here = pl.ds(i * (tok // 2), tok // 2)
        grads = dq_t[2, :, i * (rows // 2) : (i + 1) * (rows // 2)] * scale
        dq_full[here] = grads.T.astype(bf16).reshape(tok // 2, heads, hd)
        c = remote(dq_full.at[here], dq_home.at[here], swap_send.at[5 + i], swap_recv.at[5 + i], me, pg)
        c.start()
        back_q.append(c)

    @pl.when(core == 0)
    def _():
        sgrad_add(0)

        @pl.when(x > 0)
        def _():
            sgrad_send(x, at_place(z, 0, 0))

    @pl.when((x == 0) & (core == 0))
    def _():
        loop(1, nx, sgrad_add)

        @pl.when(z > 0)
        def _():
            sgrad_send(nx + z, 0)

    dq_near[...] = jnp.where(first_ret, dq_full[...], dq_band[0])
    out_near = pltpu.make_async_copy(dq_near, dq_out.at[:, 0], local_sem.at[0])
    out_near.start()

    @pl.when(me < n - 1)
    def _():
        back_copy.wait_recv()
        dkv_band[...] += back_recv[...].astype(f32)

    @pl.when(me == 0)
    def _():
        loop(1, nz, lambda zs: sgrad_add(nx + zs))
        dkv_band[:, :, 0:SINK] += sink_sum[...]

    @pl.when(core == 0)
    def _():
        sib_copy(me).wait_recv()
        dkv_own[...] += sib_part[...].astype(f32)

    def take_x(xs):
        x_copy(z, xs, x).wait_recv()
        dkv_own[...] += x_part[z, xs].astype(f32)

    loop(x + 1, nx, take_x)

    def take_z(zs):
        z_copy(zs, zs).wait_recv()
        dkv_own[...] += z_part[zs].astype(f32)

    loop(z + 1, nz, take_z)

    dkv_full[...] = dkv_own[...].astype(bf16)
    back_kv = remote(dkv_full, dkv_home, swap_send.at[8], swap_recv.at[8], me, pg)
    back_kv.start()
    dkv_out[0] = jnp.where(first_ret, dkv_full[...], dkv_band[0].astype(bf16))

    out_far = []
    for i in range(2):
        here = pl.ds(i * (tok // 2), tok // 2)
        back_q[i].wait()
        home = jnp.where(pair, dq_full[here], dq_home[here])
        dq_home[here] = jnp.where(second_ret, home, dq_band[1, here])
        c = pltpu.make_async_copy(dq_home.at[here], dq_out.at[here, 1], local_sem.at[1 + i])
        c.start()
        out_far.append(c)
    back_kv.wait()
    dkv_out[1] = jnp.where(
        second_ret, jnp.where(pair, dkv_full[...], dkv_home[...]), dkv_band[1].astype(bf16)
    )

    for c in swaps:
        c.wait_send()
    delta_copy.wait_send()

    loop(z + 1, nz, lambda zd: to_z(zd).wait_send())
    loop(x + 1, nx, lambda xd: to_x(z, xd).wait_send())

    def drain_z(zs):
        if nx == 4:
            to_x(zs, lax.rem(x + 1, nx)).wait_send()
            to_x(zs, lax.rem(x + nx - 1, nx)).wait_send()
            relay(zs).wait_send()
        else:
            for d in range(1, nx):
                to_x(zs, lax.rem(x + d, nx)).wait_send()

    loop(0, z, drain_z)
    loop(0, chip + 1 - core, lambda at: to_sib(at).wait_send())
    loop(0, 2 * chip + core, lambda blk: sib_copy(blk).wait_send())

    @pl.when(me < n - 1)
    def _():
        halo_copy.wait_send()

    @pl.when(me > 0)
    def _():
        back_copy.wait_send()
        sgrad_copy(0, sib).wait_send()

    @pl.when(me == 0)
    def _():
        loop(1, nz, lambda zd: sink_z(zd).wait_send())

    @pl.when((x == 0) & (core == 0))
    def _():
        loop(1, nx, lambda xd: sink_x(xd).wait_send())

    @pl.when(core == 0)
    def _():
        sink_copy(sib, sink_fs).wait_send()

    out_near.wait()
    for c in out_far:
        c.wait()


def shards(queries, keys, values, outputs, grads, logs, kind, sinks, windows):
    tok, _, heads, hd = queries.shape
    rows = tok * heads
    n = lax.axis_size("ctx")
    nx = min(4, n // 2)
    nz = n // 2 // nx
    lse = jnp.moveaxis(logs.astype(f32) * LOG2E, 1, 0).reshape(2, 1, rows)
    kv = jnp.moveaxis(jnp.stack([keys, values], axis=0), 2, 0)
    smem = pl.BlockSpec(memory_space=pltpu.SMEM)
    hbm = pl.BlockSpec(memory_space=pl.ANY)
    vmem = pl.BlockSpec(memory_space=pltpu.VMEM)
    V = pltpu.VMEM
    dma = pltpu.SemaphoreType.DMA
    dq, dkv = pl.pallas_call(
        functools.partial(kernel, n),
        in_specs=[smem, smem, smem, hbm, hbm, hbm, hbm, hbm],
        out_specs=[hbm, vmem],
        out_shape=[
            jax.ShapeDtypeStruct((tok, 2, heads, hd), bf16),
            jax.ShapeDtypeStruct((2, 2, tok, hd), bf16),
        ],
        scratch_shapes=[
            V((3, tok, heads, hd), bf16),
            V((3, tok, heads, hd), bf16),
            V((3, 2, tok, hd), bf16),
            V((2, tok, heads, hd), bf16),
            V((3, 1, rows), f32),
            V((3, 1, rows), f32),
            V((n, 2, tok, hd), bf16),
            V((n // 2, 2, tok, hd), f32),
            V((n, 2, tok, hd), bf16),
            V((nz, nx, 2, tok, hd), bf16),
            V((nz, 2, tok, hd), bf16),
            V((nz, 2, tok, hd), bf16),
            V((2, tok, hd), bf16),
            V((n // 2, 2, tok, hd), bf16),
            V((2, 2, tok, hd), bf16),
            V((2, 2, SINK, hd), bf16),
            V((2, 2, SINK, hd), f32),
            V((2, 2, SINK, hd), bf16),
            V((nx + nz, 2, 2, SINK, hd), bf16),
            V((2, 2, tok, hd), bf16),
            V((2, 2, tok, hd), bf16),
            V((3, hd, rows), bf16),
            V((3, hd, rows), bf16),
            V((3, rows, hd), bf16),
            V((3, rows, hd), bf16),
            V((3, hd, rows), f32),
            V((2, tok, heads, hd), bf16),
            V((tok, heads, hd), bf16),
            V((tok, heads, hd), bf16),
            V((tok, heads, hd), bf16),
            V((2, tok, hd), f32),
            V((2, 2, tok, hd), f32),
            V((2, tok, hd), bf16),
            V((2, tok, hd), bf16),
            dma((10,)),
            dma((9,)),
            dma((9,)),
            dma((n,)),
            dma((nz,)),
            dma((nz, nx)),
            dma((nz,)),
            dma((n // 2,)),
            dma((n,)),
            dma((nz, nx)),
            dma((nz,)),
            dma((nz,)),
            dma,
            dma((n // 2,)),
            dma((nz,)),
            dma((nx,)),
            dma,
            dma,
            dma,
            dma((nx + nz,)),
            dma((4,)),
        ],
        compiler_params=pltpu.CompilerParams(
            collective_id=0, has_side_effects=True, vmem_limit_bytes=60 * 2**20
        ),
        name="attention_grads",
    )(kind, sinks, windows, queries, kv, grads, outputs, lse)
    dkv = jnp.moveaxis(dkv, 0, 2)
    return dq, dkv[0], dkv[1]


def solution(mesh):
    return jax.shard_map(
        shards,
        mesh=mesh,
        in_specs=(
            P("ctx", "hg", None, None),
            P("ctx", "hg", None),
            P("ctx", "hg", None),
            P("ctx", "hg", None, None),
            P("ctx", "hg", None, None),
            P("ctx", "hg", None),
            P(),
            P(),
            P(),
        ),
        out_specs=(P("ctx", "hg", None, None), P("ctx", "hg", None), P("ctx", "hg", None)),
        check_vma=False,
    )
```

```python
import functools

import jax
import jax.numpy as jnp
from jax import lax
from jax.experimental import pallas as pl
from jax.experimental.pallas import tpu as pltpu
from jax.sharding import PartitionSpec as P

SINK = 128
MESH = pl.DeviceIdType.MESH
LOG2E = 1.4426950408889634
f32 = jnp.float32
bf16 = jnp.bfloat16


def dot(a, b):
    return lax.dot_general(a, b, (((1,), (0,)), ((), ())), preferred_element_type=f32)


def kernel(
    n,
    kind,
    sinks,
    windows,
    q_in,
    kv_in,
    do_in,
    o_in,
    lse_in,
    dq_out,
    dkv_out,
    q3,
    do3,
    kv3,
    o2,
    lse3,
    delta3,
    kv_all,
    pown,
    part,
    x_part,
    hop_part,
    z_part,
    sib_part,
    spart,
    halo,
    sink,
    sink_sum,
    sink_send,
    sink_recv,
    back_send,
    back_recv,
    q_t,
    do_t,
    q_r,
    do_r,
    dq_t,
    dq_band,
    dq_full,
    dq_near,
    dq_home,
    dkv_own,
    dkv_band,
    dkv_full,
    dkv_home,
    local_sem,
    swap_send,
    swap_recv,
    kv_recv,
    z_send,
    x_send,
    relay_send,
    fwd_send,
    part_send,
    x_recv,
    hop_recv,
    z_recv,
    sib_recv,
    spart_recv,
    sink_zs,
    sink_xs,
    sink_fs,
    sink_rs,
    sgrad_ss,
    sgrad_rs,
    edge_sem,
):
    tok = kv_all.shape[2]
    heads = q_in.shape[2]
    hd = q_in.shape[3]
    rows = tok * heads
    scale = hd ** (-0.5)
    me = lax.axis_index("ctx")
    g = lax.axis_index("hg")
    pg = g + 1 - 2 * lax.rem(g, 2)
    chips = n // 2
    chip = me // 2
    core = lax.rem(me, 2)
    nx = min(4, chips)
    nz = chips // nx
    z = chip // nx
    x = lax.rem(chip, nx)
    turn = 1 - 2 * core
    sib = me + turn
    beside = lax.rem(me - turn + n, n)
    after = lax.rem(me + 1, n)
    before = lax.rem(me + n - 1, n)

    def remote(src, dst, ss, rs, ctx, hg):
        return pltpu.make_async_remote_copy(
            src_ref=src, dst_ref=dst, send_sem=ss, recv_sem=rs, device_id=(ctx, hg), device_id_type=MESH
        )

    def at_place(pz, px, pc):
        return (pz * nx + px) * 2 + pc

    def loop(lo, hi, body):
        def one(i, _):
            body(i)
            return 0

        lax.fori_loop(lo, hi, one, 0)

    local = []
    for slot in range(2):
        local.append((kv_in.at[slot], kv3.at[slot]))
        local.append((q_in.at[:, slot], q3.at[slot]))
        local.append((do_in.at[:, slot], do3.at[slot]))
        local.append((o_in.at[:, slot], o2.at[slot]))
        local.append((lse_in.at[slot], lse3.at[slot]))
    local = [pltpu.make_async_copy(a, b, local_sem.at[i]) for i, (a, b) in enumerate(local)]
    for c in local:
        c.start()

    barrier = pltpu.get_barrier_semaphore()

    def greet(ctx, hg):
        pl.semaphore_signal(barrier, inc=1, device_id=(ctx, hg), device_id_type=MESH)

    greet(me, pg)
    greet(sib, g)
    greet(beside, g)
    for d in range(1, nz):
        greet(at_place(lax.rem(z + d, nz), x, core), g)
    for d in range(1, nx):
        greet(at_place(z, lax.rem(x + d, nx), core), g)
    pl.semaphore_wait(barrier, 1 + nz + nx)

    pieces = [
        (kv_in.at[1], kv3.at[2]),
        (lse_in.at[1], lse3.at[2]),
        (q_in.at[:, 1], q3.at[2]),
        (do_in.at[:, 1], do3.at[2]),
    ]
    swaps = [remote(a, b, swap_send.at[i], swap_recv.at[i], me, pg) for i, (a, b) in enumerate(pieces)]
    swaps[0].start()

    kinds = [kind[2 * g], kind[2 * g + 1]]
    first_ret = kinds[0] == 1
    second_ret = kinds[1] == 1
    pair = kinds[0] + kinds[1] == 1
    full_slot = jnp.where(first_ret, 0, jnp.where(pair, 1, 2))

    halo_copy = remote(kv_in.at[pl.ds(0, 2)], halo, edge_sem.at[0], edge_sem.at[1], after, g)

    @pl.when(me < n - 1)
    def _():
        halo_copy.start()

    def sink_copy(dst, sem):
        return remote(sink, sink, sem, sink_rs, dst, g)

    def sink_z(zd):
        return sink_copy(at_place(zd, 0, 0), sink_zs.at[zd])

    def sink_x(xd):
        return sink_copy(at_place(z, xd, 0), sink_xs.at[xd])

    for c in local:
        c.wait()

    @pl.when(me == 0)
    def _():
        halo[...] = jnp.zeros_like(halo)
        sink[...] = kv3[0:2, :, 0:SINK]
        loop(1, nz, lambda zd: sink_z(zd).start())

    def kv_copy(block, dst, sem):
        return remote(kv_all.at[block], kv_all.at[block], sem, kv_recv.at[block], dst, g)

    def kv_wait(block):
        kv_copy(block, sib, fwd_send.at[0]).wait_recv()

    def to_z(zd):
        return kv_copy(me, at_place(zd, x, core), z_send.at[zd])

    def to_x(zs, xd):
        return kv_copy(at_place(zs, x, core), at_place(z, xd, core), x_send.at[zs, xd])

    def to_sib(at):
        return kv_copy(2 * at + core, sib, fwd_send.at[at])

    def relay(zs):
        blk = at_place(zs, lax.rem(x - turn + nx, nx), core)
        return kv_copy(blk, at_place(z, lax.rem(x + turn + nx, nx), core), relay_send.at[zs])

    def load_head(slot):
        q = q3[slot].reshape(rows, hd)
        d = do3[slot].reshape(rows, hd)
        q_r[slot] = q
        do_r[slot] = d
        q_t[slot] = q.T
        do_t[slot] = d.T
        dq_t[slot] = jnp.zeros((hd, rows), f32)

    def row_totals(slot):
        o_t = o2[slot].reshape(rows, hd).T.astype(f32)
        delta3[slot] = jnp.sum(o_t * do_t[slot].astype(f32), axis=0, keepdims=True)

    def block(slot, acc, k, v, allowed):
        s = dot(k, q_t[slot])
        p = jnp.exp2(s * (scale * LOG2E) - lse3[slot])
        if allowed is not None:
            p = jnp.where(allowed, p, 0.0)
        dp = dot(v, do_t[slot])
        ds = (p * (dp - delta3[slot])).astype(bf16)
        dv = dot(p.astype(bf16), do_r[slot])
        dk = dot(ds, q_r[slot])
        dq_t[acc] += dot(k.T, ds)
        return dk * scale, dv

    def query_grads(acc):
        return (dq_t[acc] * scale).T.astype(bf16).reshape(tok, heads, hd)

    def gap(count, key_start):
        key = lax.broadcasted_iota(jnp.int32, (count, rows), 0) + key_start
        row = lax.broadcasted_iota(jnp.int32, (count, rows), 1) // heads
        return row - key

    def band(slot):
        window = windows[2 * g + slot]
        dist = gap(tok, 0)
        dk, dv = block(slot, slot, kv3[slot, 0], kv3[slot, 1], (dist >= 0) & (dist < window))
        dkv_band[slot, 0] = dk
        dkv_band[slot, 1] = dv
        if slot == 0:

            @pl.when(me > 0)
            def _():
                halo_copy.wait_recv()

        dk, dv = block(slot, slot, halo[slot, 0], halo[slot, 1], (dist < window - tok) & (me > 0))
        back_send[slot, 0] = dk.astype(bf16)
        back_send[slot, 1] = dv.astype(bf16)

    def band_sink(slot):
        sink_count = sinks[2 * g + slot]
        window = windows[2 * g + slot]
        key = lax.broadcasted_iota(jnp.int32, (SINK, rows), 0)
        dist = gap(SINK, 0)
        allowed = (key < sink_count) & (dist >= window - me * tok)
        dk, dv = block(slot, slot, sink[slot, 0], sink[slot, 1], allowed)
        sink_sum[slot, 0] = dk
        sink_sum[slot, 1] = dv
        dq_band[slot] = query_grads(slot)

    load_head(1)
    row_totals(1)
    delta_copy = remote(delta3.at[1], delta3.at[2], swap_send.at[4], swap_recv.at[4], me, pg)
    delta_copy.start()
    load_head(0)
    row_totals(0)
    swaps[0].wait_recv()
    for c in swaps[1:]:
        c.start()
    kv_all[me] = kv3[full_slot]
    loop(z + 1, nz, lambda zd: to_z(zd).start())
    loop(x + 1, nx, lambda xd: to_x(z, xd).start())

    @pl.when(core == 0)
    def _():
        to_sib(chip).start()

    def arrive_z(i):
        zs = z - i
        kv_wait(at_place(zs, x, core))
        if nx == 4:
            to_x(zs, lax.rem(x + 1, nx)).start()
            to_x(zs, lax.rem(x + nx - 1, nx)).start()
        else:
            for d in range(1, nx):
                to_x(zs, lax.rem(x + d, nx)).start()
        to_sib(zs * nx + x).start()

    def arrive(zs, xs):
        kv_wait(at_place(zs, xs, core))
        to_sib(zs * nx + xs).start()

    def near(zs):
        if nx == 4:
            arrive(zs, lax.rem(x - turn + nx, nx))
            relay(zs).start()
            arrive(zs, lax.rem(x + turn + nx, nx))
        else:
            for d in range(1, nx):
                arrive(zs, lax.rem(x + d, nx))

    def far(zs):
        if nx == 4:
            arrive(zs, lax.rem(x + 2, nx))

    @pl.when((x == 0) & (core == 0))
    def _():
        @pl.when(z > 0)
        def _():
            sink_copy(sib, sink_fs).wait_recv()

        loop(1, nx, lambda xd: sink_x(xd).start())

    loop(1, z + 1, arrive_z)

    @pl.when((x > 0) & (core == 0))
    def _():
        sink_copy(sib, sink_fs).wait_recv()

    @pl.when(core == 0)
    def _():
        sink_copy(sib, sink_fs).start()

    band(0)
    loop(0, x, lambda xs: arrive(z, xs))
    loop(1, z + 1, lambda i: near(z - i))
    band(1)
    loop(1, z + 1, lambda i: far(z - i))

    @pl.when(core == 1)
    def _():
        sink_copy(sib, sink_fs).wait_recv()

    band_sink(0)
    band_sink(1)

    back_copy = remote(back_send, back_recv, edge_sem.at[2], edge_sem.at[3], before, g)

    @pl.when(me > 0)
    def _():
        back_copy.start()

    def sgrad_copy(slot, dst):
        return remote(sink_send, sink_recv.at[slot], sgrad_ss, sgrad_rs.at[slot], dst, g)

    def sgrad_add(slot):
        sgrad_copy(slot, sib).wait_recv()
        sink_sum[...] += sink_recv[slot].astype(f32)

    def sgrad_send(slot, dst):
        sink_send[...] = sink_sum[...].astype(bf16)
        sgrad_copy(slot, dst).start()

    @pl.when(core == 1)
    def _():
        sgrad_send(0, sib)

    def sib_copy(dst):
        return remote(part.at[dst], sib_part, part_send.at[dst], sib_recv, sib, g)

    def spart_copy(at):
        blk = 2 * at + 1 - core
        return remote(part.at[blk], spart.at[at], part_send.at[blk], spart_recv.at[at], sib, g)

    def x_copy(zs, xs, xd):
        blk = at_place(zs, xd, core)
        return remote(
            part.at[blk], x_part.at[zs, xs], part_send.at[blk], x_recv.at[zs, xs], at_place(z, xd, core), g
        )

    def z_copy(zs, zd):
        blk = at_place(zd, x, core)
        return remote(
            part.at[blk], z_part.at[zs], part_send.at[blk], z_recv.at[zs], at_place(zd, x, core), g
        )

    def hop_copy(zs):
        blk = at_place(zs, lax.rem(x + 2, nx), core)
        to = at_place(z, lax.rem(x + turn + nx, nx), core)
        return remote(part.at[blk], hop_part.at[zs], part_send.at[blk], hop_recv.at[zs], to, g)

    def combine(at):
        zs = at // nx
        xd = lax.rem(at, nx)
        spart_copy(at).wait_recv()
        blk = 2 * at + core
        pown[at] += spart[at].astype(f32)
        straight = (zs == z) | (xd != x)
        if nx == 4:
            apart = lax.rem((xd - x) * turn + nx, nx)
            straight = (zs == z) | (apart == nx - 1)

            @pl.when((zs < z) & (apart == 2))
            def _():
                part[blk] = pown[at].astype(bf16)
                hop_copy(zs).start()

        @pl.when(straight)
        def _():
            part[blk] = pown[at].astype(bf16)
            x_copy(zs, x, xd).start()

    def hop(zs):
        if nx == 4:
            xd = lax.rem(x + turn + nx, nx)
            at = zs * nx + xd
            blk = 2 * at + core
            hop_copy(zs).wait_recv()
            part[blk] = (pown[at] + hop_part[zs].astype(f32)).astype(bf16)
            x_copy(zs, x, xd).start()

    def gather_x(zs):
        at = zs * nx + x
        blk = 2 * at + core
        for d in range(1, nx):
            if nx == 4 and d == 2:
                continue
            xs = lax.rem(x + d, nx)
            x_copy(zs, xs, x).wait_recv()
            pown[at] += x_part[zs, xs].astype(f32)
        part[blk] = pown[at].astype(bf16)
        z_copy(z, zs).start()

    for c in swaps[1:]:
        c.wait_recv()
    delta_copy.wait_recv()
    load_head(2)
    def step(at):
        theirs = 2 * at + 1 - core
        zs = at // nx
        kv_wait(theirs)
        both = pl.ds(2 * at, 2)
        keys = kv_all[both, 0].reshape(2 * tok, hd)
        values = kv_all[both, 1].reshape(2 * tok, hd)
        dk, dv = block(full_slot, 2, keys, values, None)
        part[theirs, 0] = jnp.where(core == 0, dk[tok:], dk[:tok]).astype(bf16)
        part[theirs, 1] = jnp.where(core == 0, dv[tok:], dv[:tok]).astype(bf16)
        spart_copy(at).start()
        pown[at, 0] = jnp.where(core == 0, dk[:tok], dk[tok:])
        pown[at, 1] = jnp.where(core == 0, dv[:tok], dv[tok:])

        @pl.when(at > 0)
        def _():
            combine(at - 1)

        @pl.when((lax.rem(at, nx) == 0) & (zs > 0))
        def _():
            hop(zs - 1)

        @pl.when((lax.rem(at, nx) == 0) & (zs > 1))
        def _():
            gather_x(zs - 2)

    loop(0, chip, step)

    @pl.when(core == 1)
    def _():
        kv_wait(sib)
        dk, dv = block(full_slot, 2, kv_all[sib, 0], kv_all[sib, 1], None)
        part[sib, 0] = dk.astype(bf16)
        part[sib, 1] = dv.astype(bf16)
        sib_copy(sib).start()

    @pl.when(chip > 0)
    def _():
        combine(chip - 1)

    @pl.when((z > 0) & (x == 0))
    def _():
        hop(z - 1)

    @pl.when((z > 1) & (x == 0))
    def _():
        gather_x(z - 2)

    @pl.when(z > 0)
    def _():
        gather_x(z - 1)

    dk, dv = block(full_slot, 2, kv_all[me, 0], kv_all[me, 1], gap(tok, 0) >= 0)
    dkv_own[0] = dk
    dkv_own[1] = dv


    back_q = []
    for i in range(2):
        here = pl.ds(i * (tok // 2), tok // 2)
        grads = dq_t[2, :, i * (rows // 2) : (i + 1) * (rows // 2)] * scale
        dq_full[here] = grads.T.astype(bf16).reshape(tok // 2, heads, hd)
        c = remote(dq_full.at[here], dq_home.at[here], swap_send.at[5 + i], swap_recv.at[5 + i], me, pg)
        c.start()
        back_q.append(c)

    @pl.when(core == 0)
    def _():
        sgrad_add(0)

        @pl.when(x > 0)
        def _():
            sgrad_send(x, at_place(z, 0, 0))

    @pl.when((x == 0) & (core == 0))
    def _():
        loop(1, nx, sgrad_add)

        @pl.when(z > 0)
        def _():
            sgrad_send(nx + z, 0)

    dq_near[...] = jnp.where(first_ret, dq_full[...], dq_band[0])
    out_near = pltpu.make_async_copy(dq_near, dq_out.at[:, 0], local_sem.at[0])
    out_near.start()

    @pl.when(me < n - 1)
    def _():
        back_copy.wait_recv()
        dkv_band[...] += back_recv[...].astype(f32)

    @pl.when(me == 0)
    def _():
        loop(1, nz, lambda zs: sgrad_add(nx + zs))
        dkv_band[:, :, 0:SINK] += sink_sum[...]

    @pl.when(core == 0)
    def _():
        sib_copy(me).wait_recv()
        dkv_own[...] += sib_part[...].astype(f32)

    def take_x(xs):
        x_copy(z, xs, x).wait_recv()
        dkv_own[...] += x_part[z, xs].astype(f32)

    loop(x + 1, nx, take_x)

    def take_z(zs):
        z_copy(zs, zs).wait_recv()
        dkv_own[...] += z_part[zs].astype(f32)

    loop(z + 1, nz, take_z)

    dkv_full[...] = dkv_own[...].astype(bf16)
    back_kv = remote(dkv_full, dkv_home, swap_send.at[8], swap_recv.at[8], me, pg)
    back_kv.start()
    dkv_out[0] = jnp.where(first_ret, dkv_full[...], dkv_band[0].astype(bf16))

    out_far = []
    for i in range(2):
        here = pl.ds(i * (tok // 2), tok // 2)
        back_q[i].wait()
        home = jnp.where(pair, dq_full[here], dq_home[here])
        dq_home[here] = jnp.where(second_ret, home, dq_band[1, here])
        c = pltpu.make_async_copy(dq_home.at[here], dq_out.at[here, 1], local_sem.at[1 + i])
        c.start()
        out_far.append(c)
    back_kv.wait()
    dkv_out[1] = jnp.where(
        second_ret, jnp.where(pair, dkv_full[...], dkv_home[...]), dkv_band[1].astype(bf16)
    )

    for c in swaps:
        c.wait_send()
    delta_copy.wait_send()

    loop(z + 1, nz, lambda zd: to_z(zd).wait_send())
    loop(x + 1, nx, lambda xd: to_x(z, xd).wait_send())

    def drain_z(zs):
        if nx == 4:
            to_x(zs, lax.rem(x + 1, nx)).wait_send()
            to_x(zs, lax.rem(x + nx - 1, nx)).wait_send()
            relay(zs).wait_send()
        else:
            for d in range(1, nx):
                to_x(zs, lax.rem(x + d, nx)).wait_send()

    loop(0, z, drain_z)
    loop(0, chip + 1 - core, lambda at: to_sib(at).wait_send())
    loop(0, 2 * chip + core, lambda blk: sib_copy(blk).wait_send())

    @pl.when(me < n - 1)
    def _():
        halo_copy.wait_send()

    @pl.when(me > 0)
    def _():
        back_copy.wait_send()
        sgrad_copy(0, sib).wait_send()

    @pl.when(me == 0)
    def _():
        loop(1, nz, lambda zd: sink_z(zd).wait_send())

    @pl.when((x == 0) & (core == 0))
    def _():
        loop(1, nx, lambda xd: sink_x(xd).wait_send())

    @pl.when(core == 0)
    def _():
        sink_copy(sib, sink_fs).wait_send()

    out_near.wait()
    for c in out_far:
        c.wait()


def shards(queries, keys, values, outputs, grads, logs, kind, sinks, windows):
    tok, _, heads, hd = queries.shape
    rows = tok * heads
    n = lax.axis_size("ctx")
    nx = min(4, n // 2)
    nz = n // 2 // nx
    lse = jnp.moveaxis(logs.astype(f32) * LOG2E, 1, 0).reshape(2, 1, rows)
    kv = jnp.moveaxis(jnp.stack([keys, values], axis=0), 2, 0)
    smem = pl.BlockSpec(memory_space=pltpu.SMEM)
    hbm = pl.BlockSpec(memory_space=pl.ANY)
    vmem = pl.BlockSpec(memory_space=pltpu.VMEM)
    V = pltpu.VMEM
    dma = pltpu.SemaphoreType.DMA
    dq, dkv = pl.pallas_call(
        functools.partial(kernel, n),
        in_specs=[smem, smem, smem, hbm, hbm, hbm, hbm, hbm],
        out_specs=[hbm, vmem],
        out_shape=[
            jax.ShapeDtypeStruct((tok, 2, heads, hd), bf16),
            jax.ShapeDtypeStruct((2, 2, tok, hd), bf16),
        ],
        scratch_shapes=[
            V((3, tok, heads, hd), bf16),
            V((3, tok, heads, hd), bf16),
            V((3, 2, tok, hd), bf16),
            V((2, tok, heads, hd), bf16),
            V((3, 1, rows), f32),
            V((3, 1, rows), f32),
            V((n, 2, tok, hd), bf16),
            V((n // 2, 2, tok, hd), f32),
            V((n, 2, tok, hd), bf16),
            V((nz, nx, 2, tok, hd), bf16),
            V((nz, 2, tok, hd), bf16),
            V((nz, 2, tok, hd), bf16),
            V((2, tok, hd), bf16),
            V((n // 2, 2, tok, hd), bf16),
            V((2, 2, tok, hd), bf16),
            V((2, 2, SINK, hd), bf16),
            V((2, 2, SINK, hd), f32),
            V((2, 2, SINK, hd), bf16),
            V((nx + nz, 2, 2, SINK, hd), bf16),
            V((2, 2, tok, hd), bf16),
            V((2, 2, tok, hd), bf16),
            V((3, hd, rows), bf16),
            V((3, hd, rows), bf16),
            V((3, rows, hd), bf16),
            V((3, rows, hd), bf16),
            V((3, hd, rows), f32),
            V((2, tok, heads, hd), bf16),
            V((tok, heads, hd), bf16),
            V((tok, heads, hd), bf16),
            V((tok, heads, hd), bf16),
            V((2, tok, hd), f32),
            V((2, 2, tok, hd), f32),
            V((2, tok, hd), bf16),
            V((2, tok, hd), bf16),
            dma((10,)),
            dma((9,)),
            dma((9,)),
            dma((n,)),
            dma((nz,)),
            dma((nz, nx)),
            dma((nz,)),
            dma((n // 2,)),
            dma((n,)),
            dma((nz, nx)),
            dma((nz,)),
            dma((nz,)),
            dma,
            dma((n // 2,)),
            dma((nz,)),
            dma((nx,)),
            dma,
            dma,
            dma,
            dma((nx + nz,)),
            dma((4,)),
        ],
        compiler_params=pltpu.CompilerParams(
            collective_id=0, has_side_effects=True, vmem_limit_bytes=60 * 2**20
        ),
        name="attention_grads",
    )(kind, sinks, windows, queries, kv, grads, outputs, lse)
    dkv = jnp.moveaxis(dkv, 0, 2)
    return dq, dkv[0], dkv[1]


def solution(mesh):
    return jax.shard_map(
        shards,
        mesh=mesh,
        in_specs=(
            P("ctx", "hg", None, None),
            P("ctx", "hg", None),
            P("ctx", "hg", None),
            P("ctx", "hg", None, None),
            P("ctx", "hg", None, None),
            P("ctx", "hg", None),
            P(),
            P(),
            P(),
        ),
        out_specs=(P("ctx", "hg", None, None), P("ctx", "hg", None), P("ctx", "hg", None)),
        check_vma=False,
    )
```
